32 devices in a mesh: dp: 8 (over z, core), fsdp: 4 (over y, x).
Axes of the slice: x: 2, y: 2, z: 4, core: 2. Of those that a mesh axis runs over, the one named last changes fastest.
Arguments:
- tokens: bfloat16 [8192, 2048], P(('dp', 'fsdp')), may hold values from -6 to 6
- positions: int32 [8192], P(('dp', 'fsdp')), may hold values from 0 to 1023, as said below
- cotangent: bfloat16 [8192, 2048], P(('dp', 'fsdp')), may hold values from -6 to 6
- w_attn: float32 [2048, 8192], P(('dp', 'fsdp')), may hold values from -0.125 to 0.125
- w_gate_up: float32 [2048, 16384], P(('dp', 'fsdp')), may hold values from -0.125 to 0.125
- w_down: float32 [2048, 8192], P(('dp', 'fsdp')), may hold values from -0.0625 to 0.0625
- gains: float32 [2048, 4], P(('dp', 'fsdp')), may hold values from 0.5 to 2, as said below
- m_attn: float32 [2048, 8192], P(('dp', 'fsdp')), may hold values from -56 to 56
- v_attn: float32 [2048, 8192], P(('dp', 'fsdp')), may hold values from 409.6 to 1638.4
- m_gate_up: float32 [2048, 16384], P(('dp', 'fsdp')), may hold values from -40 to 40
- v_gate_up: float32 [2048, 16384], P(('dp', 'fsdp')), may hold values from 81.92 to 327.68
- m_down: float32 [2048, 8192], P(('dp', 'fsdp')), may hold values from -56 to 56
- v_down: float32 [2048, 8192], P(('dp', 'fsdp')), may hold values from 409.6 to 1638.4
- m_gains: float32 [2048, 4], P(('dp', 'fsdp')), may hold values from -56 to 56
- v_gains: float32 [2048, 4], P(('dp', 'fsdp')), may hold values from 409.6 to 1638.4
Outputs:
- output: bfloat16 [8192, 2048], P(('dp', 'fsdp'))
- grad_tokens: float32 [8192, 2048], P(('dp', 'fsdp'))
- grad_attn: float32 [2048, 8192], P(('dp', 'fsdp'))
- grad_gate_up: float32 [2048, 16384], P(('dp', 'fsdp'))
- grad_down: float32 [2048, 8192], P(('dp', 'fsdp'))
- grad_gains: float32 [2048, 4], P(('dp', 'fsdp'))
- new_attn: float32 [2048, 8192], P(('dp', 'fsdp'))
- new_gate_up: float32 [2048, 16384], P(('dp', 'fsdp'))
- new_down: float32 [2048, 8192], P(('dp', 'fsdp'))
- new_gains: float32 [2048, 4], P(('dp', 'fsdp'))
- new_m_attn: float32 [2048, 8192], P(('dp', 'fsdp'))
- new_v_attn: float32 [2048, 8192], P(('dp', 'fsdp'))
- new_m_gate_up: float32 [2048, 16384], P(('dp', 'fsdp'))
- new_v_gate_up: float32 [2048, 16384], P(('dp', 'fsdp'))
- new_m_down: float32 [2048, 8192], P(('dp', 'fsdp'))
- new_v_down: float32 [2048, 8192], P(('dp', 'fsdp'))
- new_m_gains: float32 [2048, 4], P(('dp', 'fsdp'))
- new_v_gains: float32 [2048, 4], P(('dp', 'fsdp'))
The draws below stay inside these ranges and needn't reach their ends.
Inputs may be any that keep to these rules, and one draw needn't show every extreme that they name: Within each sequence of 1024 rows the positions count up from 0 by one and restart at 0 at most once, where a second document begins; the first sequence is one document. `gains`: Positive.
All inputs are finite; a program needn't handle non-finite values.
Results may differ from the reference program's by a relative error of at most 0.02.
Values may be sent and summed in bfloat16 or wider, within the bound.
No kernel may reach another device: no remote copies, remote signals or barrier semaphores. Data moves between devices by JAX's collectives and lax.ppermute only.
A program may use at most 296 MiB of HBM per device.

```python
import math
import jax
import jax.numpy as jnp
from jax import lax

D = 2048
HEADS = 16
HEAD_DIM = 128
FF = 8192
LENGTH = 1024
TOKENS = 8192


def draw_positions(key, part):
    seq_total = TOKENS // LENGTH
    restart = jax.random.randint(key, (seq_total,), LENGTH // 4, LENGTH)
    seq_index = jnp.arange(seq_total, dtype=jnp.int32)
    restart = jnp.where(seq_index == 0, LENGTH, restart)
    row_index = jnp.arange(LENGTH, dtype=jnp.int32)
    placed = jnp.where(row_index[None, :] < restart[:, None], row_index[None, :], row_index[None, :] - restart[:, None])
    return placed.reshape(TOKENS).astype(jnp.int32)


def draw_gains(key, part):
    first_key, second_key = jax.random.split(key)
    query_key = jax.random.uniform(first_key, (D, 2), jnp.float32, 0.6, 1.6)
    post_norm = jax.random.uniform(second_key, (D, 2), jnp.float32, 0.5, 1.5)
    return jnp.concatenate([query_key, post_norm], axis=1).astype(jnp.float32)


def spiked(array, own_key, source, target, blocks, factor):
    def block_of(dim):
        return (jnp.arange(array.shape[dim]) // (array.shape[dim] // blocks)).reshape((-1,) + (1,) * (array.ndim - 1 - dim))

    near = jax.random.permutation(own_key, blocks)[block_of(target)]
    second = (block_of(target) + blocks // 2) % blocks
    return jnp.where((block_of(source) == near) | (block_of(source) == second), factor * array, array)


def shard_levels(key, extent, cuts, smallest, high):
    level, own = 1.0, jax.random.fold_in(key, 6)
    for axis_at, parts in cuts:
        steps = jnp.exp(jax.random.uniform(jax.random.fold_in(own, axis_at), (parts,), jnp.float32, smallest / len(cuts), high / len(cuts)))
        level = level * jnp.repeat(steps, extent[axis_at] // parts).reshape([-1 if axis == axis_at else 1 for axis in range(len(extent))])
    return level


def centred(key, extent, width, bound, cuts=(), kind=jnp.bfloat16):
    drawn = width * jax.random.normal(key, extent, jnp.float32)
    if cuts:
        drawn = drawn * shard_levels(key, extent, cuts, -0.22, 0.18)
    return jnp.clip(drawn, -bound, bound).astype(kind)


def gaussian_with(rng, dims, spread, limit, cuts, heavy, kind=jnp.bfloat16):
    values = spread * jax.random.normal(rng, dims, jnp.float32)
    if cuts:
        values = values * shard_levels(rng, dims, cuts, -0.22, 0.18)
    return jnp.clip(spiked(values, jax.random.fold_in(rng, 3), *heavy), -limit, limit).astype(kind)


def setup_inputs(seed: int = 0) -> dict:
    splits = jax.random.split(jax.random.key(seed), 16)
    tokens = gaussian_with(splits[0], (TOKENS, D), 1.0, 6.0, ((0, 32),), (0, 1, 32, 2.75))
    positions = draw_positions(jax.random.fold_in(splits[15], 71), 0)
    cotangent = centred(splits[2], (TOKENS, D), 1.0, 6.0, ((0, 32),))
    w_attn = centred(splits[3], (D, 4 * D), D ** -0.5, 0.125, ((0, 32),), jnp.float32)
    w_gate_up = centred(splits[4], (D, 2 * FF), D ** -0.5, 0.125, ((0, 32),), jnp.float32)
    w_down = centred(splits[5], (D, FF), FF ** -0.5, 0.0625, ((0, 32),), jnp.float32)
    gains = draw_gains(jax.random.fold_in(splits[15], 71), 0)
    m_attn = centred(splits[7], (D, 4 * D), (0.1 * TOKENS ** 0.5), 56.0, ((0, 32),), jnp.float32)
    v_attn = jnp.clip(jnp.exp(math.log(1638.4) - 1.3862944 * jax.random.uniform(splits[8], (D, 4 * D), jnp.float32) ** shard_levels(splits[8], (D, 4 * D), ((0, 32),), -0.2, 0.2)), 409.6, 1638.4)
    m_gate_up = centred(splits[9], (D, 2 * FF), (0.07 * TOKENS ** 0.5), 40.0, ((0, 32),), jnp.float32)
    v_gate_up = jnp.clip(jnp.exp(math.log(327.68) - 1.3862944 * jax.random.uniform(splits[10], (D, 2 * FF), jnp.float32) ** shard_levels(splits[10], (D, 2 * FF), ((0, 32),), -0.2, 0.2)), 81.92, 327.68)
    m_down = centred(splits[11], (D, FF), (0.1 * TOKENS ** 0.5), 56.0, ((0, 32),), jnp.float32)
    v_down = jnp.clip(jnp.exp(math.log(1638.4) - 1.3862944 * jax.random.uniform(splits[12], (D, FF), jnp.float32) ** shard_levels(splits[12], (D, FF), ((0, 32),), -0.2, 0.2)), 409.6, 1638.4)
    m_gains = centred(splits[13], (D, 4), (0.1 * TOKENS ** 0.5), 56.0, ((0, 32),), jnp.float32)
    v_gains = jnp.clip(jnp.exp(math.log(1638.4) - 1.3862944 * jax.random.uniform(splits[14], (D, 4), jnp.float32) ** shard_levels(splits[14], (D, 4), ((0, 32),), -0.2, 0.2)), 409.6, 1638.4)
    return {"tokens": tokens, "positions": positions, "cotangent": cotangent, "w_attn": w_attn, "w_gate_up": w_gate_up, "w_down": w_down, "gains": gains, "m_attn": m_attn, "v_attn": v_attn, "m_gate_up": m_gate_up, "v_gate_up": v_gate_up, "m_down": m_down, "v_down": v_down, "m_gains": m_gains, "v_gains": v_gains}


norm_eps = 1e-06
rope_base = 500000.0
learn_rate = 0.004
gain_rate = 0.25
beta_one = 0.9
beta_two = 0.95
decay_rate = 0.1
adam_eps = 1e-08
correct_one = 1.0 - beta_one ** 2
correct_two = 1.0 - beta_two ** 2
neg_large = -1e+30

@jax.custom_vjp
def low(v):
    return lax.optimization_barrier(v.astype(jnp.bfloat16)).astype(jnp.float32)

@jax.custom_vjp
def low_back(v):
    return v

def low_keep(v):
    return (low(v), None)

def low_pass(kept, grad):
    return (grad,)

def back_keep(v):
    return (v, None)

def back_low(kept, grad):
    return (low(grad),)
low.defvjp(low_keep, low_pass)
low_back.defvjp(back_keep, back_low)

def matmul_high(left, right):
    return jnp.dot(left, right, precision=lax.Precision.HIGHEST, preferred_element_type=jnp.float32)

def rms_scale(values, gain_vec):
    return values * lax.rsqrt(lax.optimization_barrier(jnp.mean(values * values, axis=-1, keepdims=True)) + norm_eps) * gain_vec

def rope_tables(positions):
    half_dim = HEAD_DIM // 2
    frequency = jnp.exp(jnp.arange(half_dim, dtype=jnp.float32) * (-2.0 * math.log(rope_base) / HEAD_DIM))
    angles = positions.astype(jnp.float32)[:, None] * frequency[None, :]
    return (jnp.cos(angles)[:, None, :], jnp.sin(angles)[:, None, :])

def rotate(values, cosine, sine_tab):
    half_dim = values.shape[-1] // 2
    first_half = values[..., :half_dim]
    second_half = values[..., half_dim:]
    return jnp.concatenate([first_half * cosine - second_half * sine_tab, second_half * cosine + first_half * sine_tab], axis=-1)

def prepare(qkv_raw, gain_query, gain_key, cosine, sine_tab):
    amount = qkv_raw.shape[0]
    query_norm = rms_scale(qkv_raw[:, :D], gain_query).reshape(amount, HEADS, HEAD_DIM)
    key_norm = rms_scale(qkv_raw[:, D:2 * D], gain_key).reshape(amount, HEADS, HEAD_DIM)
    query_rot = rotate(query_norm, cosine, sine_tab).reshape(amount, D)
    key_rot = rotate(key_norm, cosine, sine_tab).reshape(amount, D)
    return (query_rot, key_rot, qkv_raw[:, 2 * D:])

def forward(tokens, w_attn, w_gate_up, w_down, gains, positions):
    amount = tokens.shape[0]
    attn_low = low(w_attn)
    gate_up_low = low(w_gate_up)
    down_low = low(w_down)
    gain_low = low(gains)
    cosine, sine_tab = rope_tables(positions)
    qkv_raw = low_back(matmul_high(tokens, attn_low[:, :3 * D]))
    query_rot, key_rot, value_flat = prepare(qkv_raw, gain_low[:, 0], gain_low[:, 1], cosine, sine_tab)
    query_heads = low(query_rot).reshape(amount, HEADS, HEAD_DIM)
    key_heads = low(key_rot).reshape(amount, HEADS, HEAD_DIM)
    value_heads = low(value_flat).reshape(amount, HEADS, HEAD_DIM)
    row_index = jnp.arange(amount, dtype=jnp.int32)
    first_key = row_index - positions.astype(jnp.int32)
    block_rows = math.gcd(512, amount)
    blocks = amount // block_rows
    scale = 1.0 / math.sqrt(HEAD_DIM)

    def attend(inputs):
        query_part, query_index, query_first = inputs
        raw_scores = jnp.einsum('qhd,khd->hqk', query_part, key_heads, precision=lax.Precision.HIGHEST) * scale
        raw_scores = low_back(raw_scores)
        allowed = (row_index[None, :] <= query_index[:, None]) & (row_index[None, :] >= query_first[:, None])
        masked = jnp.where(allowed[None], raw_scores, neg_large)
        top_score = lax.optimization_barrier(jnp.max(masked, axis=-1, keepdims=True))
        expo = jnp.exp(masked - top_score)
        total = lax.optimization_barrier(jnp.sum(expo, axis=-1))
        unnormed = jnp.einsum('hqk,khd->qhd', low(expo), value_heads, precision=lax.Precision.HIGHEST)
        return unnormed / jnp.transpose(total)[:, :, None]
    attended = lax.map(jax.checkpoint(attend), (query_heads.reshape(blocks, block_rows, HEADS, HEAD_DIM), row_index.reshape(blocks, block_rows), first_key.reshape(blocks, block_rows)))
    attended = low_back(low(attended.reshape(amount, D)))
    branch_attn = low_back(matmul_high(attended, attn_low[:, 3 * D:]))
    hidden_state = tokens + rms_scale(branch_attn, gain_low[:, 2])
    gate_up = low_back(matmul_high(low(hidden_state), gate_up_low))
    activation = low(jax.nn.silu(gate_up[:, :FF]) * gate_up[:, FF:])
    mlp_branch = low_back(matmul_high(activation, down_low.T))
    return hidden_state + rms_scale(mlp_branch, gain_low[:, 3])

def adamw_step(weight, gradient, moment, second, decay_coef, rate_value):
    moment_new = beta_one * moment + (1.0 - beta_one) * gradient
    second_new = beta_two * second + (1.0 - beta_two) * gradient * gradient
    step_ratio = moment_new / correct_one / (jnp.sqrt(second_new / correct_two) + adam_eps)
    return (weight * (1.0 - rate_value * decay_coef) - rate_value * step_ratio, moment_new, second_new)

def reference(tokens, positions, cotangent, w_attn, w_gate_up, w_down, gains, m_attn, v_attn, m_gate_up, v_gate_up, m_down, v_down, m_gains, v_gains):
    seq_total = TOKENS // LENGTH
    per_group = 4 if seq_total % 4 == 0 else 2 if seq_total % 2 == 0 else 1
    group_rows = per_group * LENGTH
    group_count = TOKENS // group_rows
    token_blocks = tokens.astype(jnp.float32).reshape(group_count, group_rows, D)
    position_blocks = positions.reshape(group_count, group_rows)
    cot_blocks = cotangent.astype(jnp.float32).reshape(group_count, group_rows, D)
    weights = (w_attn, w_gate_up, w_down, gains)

    def group_step(totals, inputs):
        token_part, position_part, cot_part = inputs

        def forward_part(token_in, attn_in, gate_up_in, down_in, gains_in):
            return forward(token_in, attn_in, gate_up_in, down_in, gains_in, position_part)
        result, pull_back = jax.vjp(forward_part, token_part, *weights)
        gradients = pull_back(cot_part)
        totals = tuple((running + extra for running, extra in zip(totals, gradients[1:])))
        return (totals, (result, gradients[0]))
    zero_grads = tuple((jnp.zeros(weight.shape, jnp.float32) for weight in weights))
    totals, (results, grad_blocks) = lax.scan(group_step, zero_grads, (token_blocks, position_blocks, cot_blocks))
    grad_attn, grad_gate_up, grad_down, grad_gains = totals
    new_attn, new_m_attn, new_v_attn = adamw_step(w_attn, grad_attn, m_attn, v_attn, decay_rate, learn_rate)
    new_gate_up, new_m_gate_up, new_v_gate_up = adamw_step(w_gate_up, grad_gate_up, m_gate_up, v_gate_up, decay_rate, learn_rate)
    new_down, new_m_down, new_v_down = adamw_step(w_down, grad_down, m_down, v_down, decay_rate, learn_rate)
    new_gains, new_m_gains, new_v_gains = adamw_step(gains, grad_gains, m_gains, v_gains, 0.0, gain_rate)
    output = results.reshape(TOKENS, D).astype(jnp.bfloat16)
    grad_tokens = grad_blocks.reshape(TOKENS, D)
    return (output, grad_tokens, grad_attn, grad_gate_up, grad_down, grad_gains, new_attn, new_gate_up, new_down, new_gains, new_m_attn, new_v_attn, new_m_gate_up, new_v_gate_up, new_m_down, new_v_down, new_m_gains, new_v_gains)
```

```python
import math

import jax
import jax.numpy as jnp
from jax import lax
from jax.sharding import PartitionSpec as P

HEAD_DIM = 128

norm_eps = 1e-06
rope_base = 500000.0
learn_rate = 0.004
gain_rate = 0.25
beta_one = 0.9
beta_two = 0.95
decay_rate = 0.1
adam_eps = 1e-08
correct_one = 1.0 - beta_one**2
correct_two = 1.0 - beta_two**2
neg_large = -1e30
bf16 = jnp.bfloat16
f32 = jnp.float32
GAIN_COLS = 128


def mm(left, right, dims):
    return lax.dot_general(left, right, (dims, ((), ())), preferred_element_type=f32)


def rotate(values, cosine, sine_tab):
    half_dim = values.shape[-1] // 2
    first_half = values[..., :half_dim]
    second_half = values[..., half_dim:]
    return jnp.concatenate(
        [
            first_half * cosine - second_half * sine_tab,
            second_half * cosine + first_half * sine_tab,
        ],
        axis=-1,
    )


def adamw_step(weight, gradient, moment, second, decay_coef, rate_value):
    moment_new = beta_one * moment + (1.0 - beta_one) * gradient
    second_new = beta_two * second + (1.0 - beta_two) * gradient * gradient
    step_ratio = moment_new / correct_one / (jnp.sqrt(second_new / correct_two) + adam_eps)
    return (
        weight * (1.0 - rate_value * decay_coef) - rate_value * step_ratio,
        moment_new,
        second_new,
    )


class Plane:
    def __init__(self, count):
        self.count = count
        self.square = count == 4
        self.place = lax.axis_index("fsdp")

    def swap(self, values, bit):
        return lax.ppermute(values, "fsdp", [(i, i ^ bit) for i in range(self.count)])

    def gather(self, block, axis):
        if not self.square:
            return lax.all_gather(block, "fsdp", axis=axis, tiled=True)
        other = 1 - axis
        size, cut = block.shape[axis], block.shape[other] // 2
        by_x, by_y = self.swap(block, 1), self.swap(block, 2)
        low = self.swap(lax.slice_in_dim(by_x, 0, cut, axis=other), 2)
        high = self.swap(lax.slice_in_dim(by_y, cut, 2 * cut, axis=other), 1)
        shape = list(block.shape)
        shape[axis] = size * 4
        out = jnp.zeros(shape, block.dtype)
        for part, bit, offset in ((block, 0, 0), (by_x, 1, 0), (by_y, 2, 0), (low, 3, 0), (high, 3, cut)):
            start = [0, 0]
            start[axis] = (self.place ^ bit) * size
            start[other] = offset
            out = lax.dynamic_update_slice(out, part, start)
        return out

    def scatter(self, partial, axis):
        if not self.square:
            return lax.psum_scatter(
                partial, "fsdp", scatter_dimension=axis, tiled=True
            ).astype(f32)
        other = 1 - axis
        size, cut = partial.shape[axis] // 4, partial.shape[other] // 2
        place = self.place

        def piece(bit, offset):
            start = [0, 0]
            start[axis] = (place ^ bit) * size
            start[other] = offset
            extent = [0, 0]
            extent[axis] = size
            extent[other] = cut
            return lax.dynamic_slice(partial, start, extent)

        halves = []
        for offset, first, second in ((0, 1, 2), (cut, 2, 1)):
            mine = self.swap(piece(first, offset), first)
            relay = self.swap(piece(3, offset), first)
            relay = (piece(second, offset).astype(f32) + relay.astype(f32)).astype(bf16)
            halves.append(
                piece(0, offset).astype(f32) + mine.astype(f32) + self.swap(relay, second).astype(f32)
            )
        return jnp.concatenate(halves, axis=other)

    def total(self, values):
        if not self.square:
            return lax.psum(values, "fsdp")
        return values + self.swap(values, 1) + self.swap(values, 2) + self.swap(values, 3)

    def gather_small(self, values):
        if not self.square:
            return lax.all_gather(values, "fsdp", axis=0, tiled=True)
        parts = [values] + [self.swap(values, bit) for bit in (1, 2, 3)]
        return jnp.concatenate(
            [
                lax.select_n(self.place ^ j, *parts)
                for j in range(4)
            ],
            axis=0,
        )


def per_device(
    tokens,
    positions,
    cotangent,
    w_attn,
    w_gate_up,
    w_down,
    gains,
    m_attn,
    v_attn,
    m_gate_up,
    v_gate_up,
    m_down,
    v_down,
    m_gains,
    v_gains,
):
    rows, width = tokens.shape
    owned = w_attn.shape[0]
    hidden = w_down.shape[1]
    count = lax.axis_size("fsdp")
    plane = Plane(count)
    place = plane.place
    length = rows * count
    part = width // count
    heads = part // HEAD_DIM
    wide = hidden // count
    scale = 1.0 / math.sqrt(HEAD_DIM)

    def spread(weight, groups, extra=None):
        columns = weight.shape[1] // (groups * count)
        block = (
            weight.astype(bf16)
            .reshape(owned, groups, count, columns)
            .transpose(2, 0, 1, 3)
            .reshape(count, owned, groups * columns)
        )
        if extra is not None:
            block = jnp.concatenate(
                [block, jnp.broadcast_to(extra[None], (count,) + extra.shape)], axis=2
            )
        block = block.reshape(count * owned, block.shape[2])
        return lax.all_to_all(block, "fsdp", 0, 0, tiled=True)

    gain_block = jnp.pad(gains.astype(bf16), ((0, 0), (0, GAIN_COLS - gains.shape[1])))
    attn_all = lax.all_gather(spread(w_attn, 4, gain_block), "dp", axis=0, tiled=True)
    gate_up_all = lax.all_gather(spread(w_gate_up, 2), "dp", axis=0, tiled=True)
    down_all = lax.all_gather(spread(w_down, 1), "dp", axis=0, tiled=True)
    qkv_weight = attn_all[:, : 3 * part]
    out_weight = attn_all[:, 3 * part : 4 * part]
    gain_values = attn_all[:, 4 * part : 4 * part + 4].astype(f32)
    gain_part = lax.dynamic_slice_in_dim(gain_values, place * part, part, 0)

    token_full = plane.gather(tokens, 0)
    position_full = plane.gather_small(positions)
    cot_part = lax.all_to_all(
        cotangent.reshape(rows, count, part).transpose(1, 0, 2).reshape(count * rows, part),
        "fsdp",
        0,
        0,
        tiled=True,
    ).astype(f32)

    half_dim = HEAD_DIM // 2
    frequency = jnp.exp(
        jnp.arange(half_dim, dtype=f32) * (-2.0 * math.log(rope_base) / HEAD_DIM)
    )
    angles = position_full.astype(f32)[:, None] * frequency[None, :]
    cosine, sine_tab = jnp.cos(angles)[:, None, :], jnp.sin(angles)[:, None, :]
    row_index = jnp.arange(length, dtype=jnp.int32)
    first_key = row_index - position_full
    allowed = (row_index[None, :] <= row_index[:, None]) & (
        row_index[None, :] >= first_key[:, None]
    )

    qkv = mm(token_full, qkv_weight, ((1,), (0,)))
    query_raw, key_raw, value_raw = qkv[:, :part], qkv[:, part : 2 * part], qkv[:, 2 * part :]
    squares = plane.total(
        jnp.stack([jnp.sum(query_raw * query_raw, axis=1), jnp.sum(key_raw * key_raw, axis=1)])
    )
    inverse = lax.rsqrt(squares / width + norm_eps)
    query_inv, key_inv = inverse[0][:, None], inverse[1][:, None]
    query_hat, key_hat = query_raw * query_inv, key_raw * key_inv

    def turned(values, gain):
        return (
            rotate((values * gain[None, :]).reshape(length, heads, HEAD_DIM), cosine, sine_tab)
            .astype(bf16)
        )

    query = turned(query_hat, gain_part[:, 0])
    key = turned(key_hat, gain_part[:, 1])
    value = value_raw.astype(bf16).reshape(length, heads, HEAD_DIM)

    def score():
        scores = jnp.einsum("qhd,khd->hqk", query, key, preferred_element_type=f32) * scale
        return jnp.where(allowed[None], scores, neg_large)

    scores = score()
    top = jnp.max(scores, axis=-1)
    weights = jnp.exp(scores - top[:, :, None])
    denom = jnp.sum(weights, axis=-1)
    attended = jnp.einsum(
        "hqk,khd->qhd", weights.astype(bf16), value, preferred_element_type=f32
    ) / jnp.transpose(denom)[:, :, None]
    attended_low = attended.reshape(length, part).astype(bf16)
    attended_full = plane.gather(attended_low, 1)

    branch = mm(attended_full, out_weight, ((1,), (0,)))
    branch_inv = lax.rsqrt(plane.total(jnp.sum(branch * branch, axis=1)) / width + norm_eps)[:, None]
    branch_hat = branch * branch_inv
    token_part = lax.dynamic_slice_in_dim(token_full, place * part, part, 1).astype(f32)
    hidden_low = (token_part + branch_hat * gain_part[None, :, 2]).astype(bf16)
    hidden_full = plane.gather(hidden_low, 1)

    gate_up = mm(hidden_full, gate_up_all, ((1,), (0,)))
    gate, up = gate_up[:, :wide], gate_up[:, wide:]
    activ = (jax.nn.silu(gate) * up).astype(bf16)
    mlp = plane.scatter(mm(activ, down_all, ((1,), (1,))).astype(bf16), 0)
    mlp_inv = lax.rsqrt(jnp.mean(mlp * mlp, axis=1, keepdims=True) + norm_eps)
    mlp_hat = mlp * mlp_inv
    hidden_rows = lax.dynamic_slice_in_dim(hidden_full, place * rows, rows, 0).astype(f32)
    output = (hidden_rows + mlp_hat * gain_values[None, :, 3]).astype(bf16)

    grad_out = cotangent.astype(f32)
    scaled = grad_out * gain_values[None, :, 3]
    grad_mlp = mlp_inv * (scaled - mlp_hat * jnp.mean(scaled * mlp_hat, axis=1, keepdims=True))
    grad_gain_mlp = jnp.sum(grad_out * mlp_hat, axis=0)
    grad_mlp_full = plane.gather(grad_mlp.astype(bf16), 0)

    def reduced(partial, groups):
        mine = lax.psum_scatter(partial, "dp", scatter_dimension=0, tiled=True)
        got = lax.all_to_all(mine, "fsdp", 0, 0, tiled=True)
        columns = partial.shape[1] // groups
        return (
            got.reshape(count, owned, groups, columns)
            .transpose(1, 2, 0, 3)
            .reshape(owned, groups * count * columns)
            .astype(f32)
        )

    grad_down = reduced(mm(grad_mlp_full, activ, ((0,), (0,))).astype(bf16), 1)
    grad_activ = mm(grad_mlp_full, down_all, ((1,), (0,)))
    sigmoid = jax.nn.sigmoid(gate)
    grad_gate = grad_activ * up * sigmoid * (1.0 + gate * (1.0 - sigmoid))
    grad_up = grad_activ * (gate * sigmoid)
    grad_gate_up_low = jnp.concatenate([grad_gate, grad_up], axis=1).astype(bf16)
    grad_gate_up = reduced(mm(hidden_full, grad_gate_up_low, ((0,), (0,))).astype(bf16), 2)
    grad_hidden = cot_part + plane.scatter(
        mm(grad_gate_up_low, gate_up_all, ((1,), (1,))).astype(bf16), 1
    )

    scaled = grad_hidden * gain_part[None, :, 2]
    grad_gain_attn = jnp.sum(grad_hidden * branch_hat, axis=0)
    inner = plane.total(jnp.sum(scaled * branch_hat, axis=1))[:, None] / width
    grad_branch = (branch_inv * (scaled - branch_hat * inner)).astype(bf16)
    grad_out_weight = mm(attended_full, grad_branch, ((0,), (0,))).astype(bf16)
    grad_att = (
        plane.scatter(mm(grad_branch, out_weight, ((1,), (1,))).astype(bf16), 1)
        .astype(bf16)
        .reshape(length, heads, HEAD_DIM)
    )
    delta = jnp.transpose(jnp.sum(grad_att.astype(f32) * attended, axis=-1))
    scores = score()
    prob = jnp.exp(scores - (top + jnp.log(denom))[:, :, None])
    weight_low = jnp.exp(scores - top[:, :, None]).astype(bf16)
    grad_probs = jnp.einsum("qhd,khd->hqk", grad_att, value, preferred_element_type=f32)
    grad_scores = (prob * (grad_probs - delta[:, :, None])).astype(bf16)
    grad_query = (
        jnp.einsum("hqk,khd->qhd", grad_scores, key, preferred_element_type=f32) * scale
    )
    grad_key = (
        jnp.einsum("hqk,qhd->khd", grad_scores, query, preferred_element_type=f32) * scale
    )
    scaled_rows = (grad_att.astype(f32) / jnp.transpose(denom)[:, :, None]).astype(bf16)
    grad_value = jnp.einsum("hqk,qhd->khd", weight_low, scaled_rows, preferred_element_type=f32)

    query_back = rotate(grad_query, cosine, -sine_tab).reshape(length, part)
    key_back = rotate(grad_key, cosine, -sine_tab).reshape(length, part)
    grad_gain_query = jnp.sum(query_back * query_hat, axis=0)
    grad_gain_key = jnp.sum(key_back * key_hat, axis=0)
    query_back = query_back * gain_part[None, :, 0]
    key_back = key_back * gain_part[None, :, 1]
    inner = plane.total(
        jnp.stack([jnp.sum(query_back * query_hat, axis=1), jnp.sum(key_back * key_hat, axis=1)])
    ) / width
    grad_qkv_low = jnp.concatenate(
        [
            query_inv * (query_back - query_hat * inner[0][:, None]),
            key_inv * (key_back - key_hat * inner[1][:, None]),
            grad_value.reshape(length, part),
        ],
        axis=1,
    ).astype(bf16)
    grad_qkv_weight = mm(token_full, grad_qkv_low, ((0,), (0,))).astype(bf16)

    own_gains = jnp.stack([grad_gain_query, grad_gain_key, grad_gain_attn], axis=1)
    gain_cols = lax.dynamic_update_slice(
        jnp.zeros((width, GAIN_COLS), f32), own_gains, (place * part, 0)
    )
    gain_cols = lax.dynamic_update_slice(gain_cols, grad_gain_mlp[:, None], (0, 3))
    attn_partial = jnp.concatenate(
        [grad_qkv_weight, grad_out_weight, gain_cols.astype(bf16)], axis=1
    )
    mine = lax.psum_scatter(attn_partial, "dp", scatter_dimension=0, tiled=True)
    got = lax.all_to_all(mine, "fsdp", 0, 0, tiled=True).reshape(count, owned, 4 * part + GAIN_COLS)
    grad_attn = (
        got[:, :, : 4 * part]
        .reshape(count, owned, 4, part)
        .transpose(1, 2, 0, 3)
        .reshape(owned, 4 * width)
        .astype(f32)
    )
    grad_gains = jnp.sum(got[:, :, 4 * part : 4 * part + 4].astype(f32), axis=0)

    back = mm(grad_qkv_low, qkv_weight, ((1,), (1,)))
    own_cols = lax.dynamic_slice_in_dim(back, place * part, part, 1) + grad_hidden
    back = lax.dynamic_update_slice(back, own_cols, (0, place * part))
    grad_tokens = plane.scatter(back.astype(bf16), 0)

    new_attn, new_m_attn, new_v_attn = adamw_step(
        w_attn, grad_attn, m_attn, v_attn, decay_rate, learn_rate
    )
    new_gate_up, new_m_gate_up, new_v_gate_up = adamw_step(
        w_gate_up, grad_gate_up, m_gate_up, v_gate_up, decay_rate, learn_rate
    )
    new_down, new_m_down, new_v_down = adamw_step(
        w_down, grad_down, m_down, v_down, decay_rate, learn_rate
    )
    new_gains, new_m_gains, new_v_gains = adamw_step(
        gains, grad_gains, m_gains, v_gains, 0.0, gain_rate
    )
    return (
        output,
        grad_tokens,
        grad_attn,
        grad_gate_up,
        grad_down,
        grad_gains,
        new_attn,
        new_gate_up,
        new_down,
        new_gains,
        new_m_attn,
        new_v_attn,
        new_m_gate_up,
        new_v_gate_up,
        new_m_down,
        new_v_down,
        new_m_gains,
        new_v_gains,
    )


def solution(mesh):
    matrix, vector = P(("dp", "fsdp"), None), P(("dp", "fsdp"))
    in_specs = (matrix, vector) + (matrix,) * 13
    return jax.shard_map(
        per_device, mesh=mesh, in_specs=in_specs, out_specs=(matrix,) * 18, check_vma=False
    )
```

```python
import functools
import math

import jax
import jax.numpy as jnp
from jax import lax
from jax.experimental import pallas as pl
from jax.experimental.pallas import tpu as pltpu
from jax.experimental.layout import Layout, with_layout_constraint
from jax.sharding import Mesh
from jax.sharding import PartitionSpec as P

HEAD_DIM = 128

norm_eps = 1e-06
rope_base = 500000.0
learn_rate = 0.004
gain_rate = 0.25
beta_one = 0.9
beta_two = 0.95
decay_rate = 0.1
adam_eps = 1e-08
correct_one = 1.0 - beta_one**2
correct_two = 1.0 - beta_two**2
neg_large = -1e30
bf16 = jnp.bfloat16
f32 = jnp.float32
GAIN_COLS = 128
TILE = 512


def mm(left, right, dims):
    return lax.dot_general(left, right, (dims, ((), ())), preferred_element_type=f32)


def adamw_step(weight, gradient, moment, second, decay_coef, rate_value):
    moment_new = beta_one * moment + (1.0 - beta_one) * gradient
    second_new = beta_two * second + (1.0 - beta_two) * gradient * gradient
    step_ratio = moment_new / correct_one / (jnp.sqrt(second_new / correct_two) + adam_eps)
    return (
        weight * (1.0 - rate_value * decay_coef) - rate_value * step_ratio,
        moment_new,
        second_new,
    )


def spread_body(tile, *refs):
    out = refs[-1]
    if tile:
        for i in range(refs[0].shape[1] // tile):
            for g, ref in enumerate(refs[:-1]):
                start = (i * len(refs[:-1]) + g) * tile
                out[:, start : start + tile] = ref[:, i * tile : (i + 1) * tile].astype(bf16)
        return
    start = 0
    for ref in refs[:-1]:
        out[:, start : start + ref.shape[1]] = ref[...].astype(bf16)
        start += ref.shape[1]


def spread_kernel(weight, groups, count, extra, tile):
    owned, columns = weight.shape
    size = columns // (groups * count)
    specs = [
        pl.BlockSpec((owned, size), lambda f, g=g: (0, g * count + f)) for g in range(groups)
    ]
    operands = [weight] * groups
    wide = groups * size
    if extra is not None:
        specs.append(pl.BlockSpec(extra.shape, lambda f: (0, 0)))
        operands.append(extra)
        wide += extra.shape[1]
    return pl.pallas_call(
        functools.partial(spread_body, tile),
        grid=(count,),
        in_specs=specs,
        out_specs=pl.BlockSpec((owned, wide), lambda f: (f, 0)),
        out_shape=jax.ShapeDtypeStruct((count * owned, wide), bf16),
        compiler_params=pltpu.CompilerParams(vmem_limit_bytes=40 * 1024 * 1024),
        cost_estimate=pl.CostEstimate(
            flops=0, bytes_accessed=6 * owned * columns, transcendentals=0
        ),
    )(*operands)


def adamw_body(tile, *refs):
    grad_in, weight, moment, second, grad_out, new_weight, new_moment, new_second = refs
    if tile:
        groups = grad_in.shape[1] // weight.shape[1]
        for i in range(weight.shape[1] // tile):
            start = pl.multiple_of((i * groups + pl.program_id(1)) * tile, tile)
            grad_out[:, i * tile : (i + 1) * tile] = grad_in[:, pl.ds(start, tile)].astype(f32)
    else:
        grad_out[...] = grad_in[...].astype(f32)
    new_weight[...], new_moment[...], new_second[...] = adamw_step(
        weight[...], grad_out[...], moment[...], second[...], decay_rate, learn_rate
    )


def adamw_kernel(gradient, weight, moment, second, groups, count, tile=0):
    owned, columns = weight.shape
    size = columns // (groups * count)
    whole = pl.BlockSpec((owned, size), lambda f, g: (0, g * count + f))
    if tile:
        grad_spec = pl.BlockSpec((owned, groups * size), lambda f, g: (f, 0))
    else:
        grad_spec = pl.BlockSpec((owned, size), lambda f, g: (f, g))
    return pl.pallas_call(
        functools.partial(adamw_body, tile),
        grid=(count, groups),
        in_specs=[grad_spec, whole, whole, whole],
        out_specs=[whole] * 4,
        out_shape=[jax.ShapeDtypeStruct(weight.shape, f32)] * 4,
        compiler_params=pltpu.CompilerParams(vmem_limit_bytes=40 * 1024 * 1024),
        cost_estimate=pl.CostEstimate(
            flops=12 * owned * columns, bytes_accessed=30 * owned * columns, transcendentals=0
        ),
    )(gradient, weight, moment, second)


def dot(left, right, left_dim, right_dim):
    return lax.dot_general(
        left, right, (((left_dim,), (right_dim,)), ((), ())), preferred_element_type=f32
    )


def visible(first_ref, low, high):
    shape = (high - low, high)
    row = lax.broadcasted_iota(jnp.int32, shape, 0) + low
    column = lax.broadcasted_iota(jnp.int32, shape, 1)
    return (column <= row) & (column >= first_ref[low:high, :])


def attend_body(block, scale, *refs):
    query_in, key_in, value_in, inverse, gain, cosine, sine, first = refs[:8]
    query_out, key_out, value_out, attended, lse = refs[8:]

    def turned(values, column):
        normed = values * inverse[:, column : column + 1] * gain[column : column + 1, :]
        return (normed * cosine[...] + pltpu.roll(normed, HEAD_DIM // 2, 1) * sine[...]).astype(bf16)

    query_out[...] = turned(query_in[...], 0)
    key_out[...] = turned(key_in[...], 1)
    value_out[...] = value_in[...].astype(bf16)
    for low in range(0, query_in.shape[0], block):
        high = low + block
        scores = dot(query_out[low:high, :], key_out[:high, :], 1, 1) * scale
        scores = jnp.where(visible(first, low, high), scores, neg_large)
        top = jnp.max(scores, axis=1, keepdims=True)
        weights = jnp.exp(scores - top)
        denom = jnp.sum(weights, axis=1, keepdims=True)
        attended[low:high, :] = (
            dot(weights.astype(bf16), value_out[:high, :], 1, 0) / denom
        ).astype(bf16)
        lse[0, low:high, :] = top + jnp.log(denom)


def attend_back_body(block, scale, *refs):
    query, key, value, attended, grad_att, lse = refs[:6]
    query_in, key_in, inverse, gain, cosine, sine, first = refs[6:13]
    query_grad, key_grad, value_grad, gain_grad, inner = refs[13:18]
    grad_low, key_sum, value_sum = refs[18:]
    grad_low[...] = grad_att[...].astype(bf16)
    delta = jnp.sum(
        grad_low[...].astype(f32) * attended[...].astype(f32), axis=1, keepdims=True
    )
    key_sum[...] = jnp.zeros_like(key_sum)
    value_sum[...] = jnp.zeros_like(value_sum)
    for low in range(0, query.shape[0], block):
        high = low + block
        scores = dot(query[low:high, :], key[:high, :], 1, 1) * scale
        prob = jnp.where(
            visible(first, low, high), jnp.exp(scores - lse[0, low:high, :]), 0.0
        )
        grad_prob = dot(grad_low[low:high, :], value[:high, :], 1, 1)
        grad_scores = (prob * (grad_prob - delta[low:high, :])).astype(bf16)
        query_grad[low:high, :] = dot(grad_scores, key[:high, :], 1, 0) * scale
        key_sum[:high, :] += dot(grad_scores, query[low:high, :], 0, 0)
        value_sum[:high, :] += dot(prob.astype(bf16), grad_low[low:high, :], 0, 0)
    value_grad[...] = value_sum[...].astype(bf16)
    lane = lax.broadcasted_iota(jnp.int32, inner.shape, 1)

    @pl.when(pl.program_id(0) == 0)
    def _():
        inner[...] = jnp.zeros_like(inner)

    gain_grad[...] = jnp.zeros_like(gain_grad)
    for column, turned, raw, out in (
        (0, query_grad[...], query_in, query_grad),
        (1, key_sum[...] * scale, key_in, key_grad),
    ):
        back = turned * cosine[...] - pltpu.roll(turned, HEAD_DIM // 2, 1) * sine[...]
        hat = raw[...] * inverse[:, column : column + 1]
        gain_grad[column : column + 1, :] = jnp.sum(back * hat, axis=0, keepdims=True)
        back = back * gain[column : column + 1, :]
        out[...] = back
        inner[...] += jnp.where(
            lane == column, jnp.sum(back * hat, axis=1, keepdims=True), 0.0
        )


def attend_kernels(length, heads):
    block = math.gcd(length, 256)
    scale = 1.0 / math.sqrt(HEAD_DIM)
    part = heads * HEAD_DIM

    def own(shift=0):
        return pl.BlockSpec((length, HEAD_DIM), lambda h: (0, h + shift))

    def same(width):
        return pl.BlockSpec((length, width), lambda h: (0, 0))

    gain_spec = pl.BlockSpec((8, HEAD_DIM), lambda h: (0, h))
    lse_spec = pl.BlockSpec((1, length, 1), lambda h: (h, 0, 0))
    tables = [same(2), gain_spec, same(HEAD_DIM), same(HEAD_DIM), same(1)]
    low_shape = jax.ShapeDtypeStruct((length, part), bf16)
    wide_shape = jax.ShapeDtypeStruct((length, part), f32)
    work = 2 * heads * length * length * HEAD_DIM
    params = pltpu.CompilerParams(vmem_limit_bytes=48 * 1024 * 1024)

    def forward(qkv, *rest):
        return pl.pallas_call(
            functools.partial(attend_body, block, scale),
            grid=(heads,),
            in_specs=[own(), own(heads), own(2 * heads)] + tables,
            out_specs=[own()] * 4 + [lse_spec],
            out_shape=[low_shape] * 4 + [jax.ShapeDtypeStruct((heads, length, 1), f32)],
            compiler_params=params,
            cost_estimate=pl.CostEstimate(
                flops=2 * work, bytes_accessed=20 * length * part, transcendentals=0
            ),
        )(qkv, qkv, qkv, *rest)

    def backward(query, key, value, attended, grad_att, lse, qkv, *rest):
        return pl.pallas_call(
            functools.partial(attend_back_body, block, scale),
            grid=(heads,),
            in_specs=[own()] * 5 + [lse_spec, own(), own(heads)] + tables,
            out_specs=[own()] * 3 + [gain_spec, same(HEAD_DIM)],
            out_shape=[
                wide_shape,
                wide_shape,
                low_shape,
                jax.ShapeDtypeStruct((8, part), f32),
                jax.ShapeDtypeStruct((length, HEAD_DIM), f32),
            ],
            scratch_shapes=[
                pltpu.VMEM((length, HEAD_DIM), bf16),
                pltpu.VMEM((length, HEAD_DIM), f32),
                pltpu.VMEM((length, HEAD_DIM), f32),
            ],
            compiler_params=params,
            cost_estimate=pl.CostEstimate(
                flops=5 * work, bytes_accessed=30 * length * part, transcendentals=0
            ),
        )(query, key, value, attended, grad_att, lse, qkv, qkv, *rest)

    return forward, backward


def qkv_back_body(query_grad, key_grad, value_grad, raw, inverse, inner, out):
    part = query_grad.shape[1]
    for column, grad in ((0, query_grad), (1, key_grad)):
        scale = inverse[:, column : column + 1]
        hat = raw[:, column * part : (column + 1) * part] * scale
        out[:, column * part : (column + 1) * part] = (
            scale * (grad[...] - hat * inner[:, column : column + 1])
        ).astype(bf16)
    out[:, 2 * part :] = value_grad[...]


def qkv_back(query_grad, key_grad, value_grad, qkv, inverse, inner):
    length, part = query_grad.shape
    rows = math.gcd(length, 256)

    def spec(width):
        return pl.BlockSpec((rows, width), lambda i: (i, 0))

    return pl.pallas_call(
        qkv_back_body,
        grid=(length // rows,),
        in_specs=[spec(part)] * 3 + [spec(2 * part), spec(2), spec(2)],
        out_specs=spec(3 * part),
        out_shape=jax.ShapeDtypeStruct((length, 3 * part), bf16),
        compiler_params=pltpu.CompilerParams(vmem_limit_bytes=40 * 1024 * 1024),
        cost_estimate=pl.CostEstimate(
            flops=8 * length * part, bytes_accessed=24 * length * part, transcendentals=0
        ),
    )(query_grad, key_grad, value_grad, qkv, inverse, inner)


def attn_grad_body(token, grad_qkv, attended, grad_branch, gain, out):
    wide, part = grad_qkv.shape[1], grad_branch.shape[1]
    out[:, :wide] = dot(token[...], grad_qkv[...], 1, 0).astype(bf16)
    out[:, wide : wide + part] = dot(attended[...], grad_branch[...], 1, 0).astype(bf16)
    gains = jnp.concatenate(
        [gain[...], jnp.zeros((GAIN_COLS - gain.shape[0], gain.shape[1]), f32)], axis=0
    )
    out[:, wide + part :] = jnp.transpose(gains).astype(bf16)


def attn_grad(token, grad_qkv, attended, grad_branch, gain):
    width, length = token.shape
    rows = math.gcd(width, 512)
    columns = grad_qkv.shape[1] + grad_branch.shape[1] + GAIN_COLS

    def row_spec(wide):
        return pl.BlockSpec((rows, wide), lambda i: (i, 0))

    def whole(array):
        return pl.BlockSpec(array.shape, lambda i: (0, 0))

    return pl.pallas_call(
        attn_grad_body,
        grid=(width // rows,),
        in_specs=[
            row_spec(length),
            whole(grad_qkv),
            row_spec(length),
            whole(grad_branch),
            pl.BlockSpec((gain.shape[0], rows), lambda i: (0, i)),
        ],
        out_specs=row_spec(columns),
        out_shape=jax.ShapeDtypeStruct((width, columns), bf16),
        compiler_params=pltpu.CompilerParams(vmem_limit_bytes=48 * 1024 * 1024),
        cost_estimate=pl.CostEstimate(
            flops=2 * width * length * columns,
            bytes_accessed=6 * width * length,
            transcendentals=0,
        ),
    )(token, grad_qkv, attended, grad_branch, gain)


def token_grad_body(place, grad_qkv, weight, grad_hidden, out):
    own = (pl.program_id(0) == place[0]).astype(f32)
    out[...] = (dot(grad_qkv[...], weight[...], 1, 1) + own * grad_hidden[...]).astype(bf16)


def token_grad(place, grad_qkv, weight, grad_hidden):
    length, wide = grad_qkv.shape
    width, part = weight.shape[0], grad_hidden.shape[1]
    return pl.pallas_call(
        token_grad_body,
        grid_spec=pltpu.PrefetchScalarGridSpec(
            num_scalar_prefetch=1,
            grid=(width // part,),
            in_specs=[
                pl.BlockSpec((length, wide), lambda j, place: (0, 0)),
                pl.BlockSpec((part, wide), lambda j, place: (j, 0)),
                pl.BlockSpec((length, part), lambda j, place: (0, 0)),
            ],
            out_specs=pl.BlockSpec((length, part), lambda j, place: (0, j)),
        ),
        out_shape=jax.ShapeDtypeStruct((length, width), bf16),
        compiler_params=pltpu.CompilerParams(vmem_limit_bytes=48 * 1024 * 1024),
        cost_estimate=pl.CostEstimate(
            flops=2 * width * length * wide, bytes_accessed=8 * width * length, transcendentals=0
        ),
    )(place, grad_qkv, weight, grad_hidden)


def gate_up_body(hidden, weight, both, activ):
    value = dot(hidden[...], weight[...], 1, 0)
    gate, up = value[:, :TILE], value[:, TILE:]
    sigmoid = jax.nn.sigmoid(gate)
    silu = gate * sigmoid
    activ[...] = (silu * up).astype(bf16)
    both[:, :TILE] = up * sigmoid * (1.0 + gate * (1.0 - sigmoid))
    both[:, TILE:] = silu


def gate_up_back_body(grad_mlp, weight, both, out):
    grad = dot(grad_mlp[...], weight[...], 1, 0)
    for start in (0, TILE):
        out[:, start : start + TILE] = (grad * both[:, start : start + TILE]).astype(bf16)


def gate_up_kernels(length, width, wide):
    params = pltpu.CompilerParams(vmem_limit_bytes=48 * 1024 * 1024)
    rows_spec = pl.BlockSpec((length, width), lambda j: (0, 0))

    def columns(rows, size):
        return pl.BlockSpec((rows, size), lambda j: (0, j))

    def forward(hidden, weight):
        return pl.pallas_call(
            gate_up_body,
            grid=(wide // TILE,),
            in_specs=[rows_spec, columns(width, 2 * TILE)],
            out_specs=[columns(length, 2 * TILE), columns(length, TILE)],
            out_shape=[
                jax.ShapeDtypeStruct((length, 2 * wide), f32),
                jax.ShapeDtypeStruct((length, wide), bf16),
            ],
            compiler_params=params,
            cost_estimate=pl.CostEstimate(
                flops=4 * length * width * wide,
                bytes_accessed=10 * length * wide + 4 * width * wide,
                transcendentals=0,
            ),
        )(hidden, weight)

    def backward(grad_mlp, weight, both):
        return pl.pallas_call(
            gate_up_back_body,
            grid=(wide // TILE,),
            in_specs=[rows_spec, columns(width, TILE), columns(length, 2 * TILE)],
            out_specs=columns(length, 2 * TILE),
            out_shape=jax.ShapeDtypeStruct((length, 2 * wide), bf16),
            compiler_params=params,
            cost_estimate=pl.CostEstimate(
                flops=2 * length * width * wide,
                bytes_accessed=12 * length * wide + 2 * width * wide,
                transcendentals=0,
            ),
        )(grad_mlp, weight, both)

    return forward, backward


FSDP, DP = ("y", "x"), ("z", "core")


def order_body(values, other, out):
    pass


def order(values, other):
    anywhere = pl.BlockSpec(memory_space=pl.ANY)
    return pl.pallas_call(
        order_body,
        in_specs=[anywhere, anywhere],
        out_specs=anywhere,
        out_shape=jax.ShapeDtypeStruct(values.shape, values.dtype),
        input_output_aliases={0: 0},
    )(values, other)


class Plane:
    def __init__(self, count):
        self.count = count
        self.square = count == 4
        self.place = lax.axis_index(FSDP)

    def swap(self, values, bit):
        return lax.ppermute(values, FSDP, [(i, i ^ bit) for i in range(self.count)])

    def gather(self, block, axis):
        if not self.square:
            return lax.all_gather(block, FSDP, axis=axis, tiled=True)
        other = 1 - axis
        size, cut = block.shape[axis], block.shape[other] // 2
        by_x, by_y = self.swap(block, 1), self.swap(block, 2)
        low = self.swap(lax.slice_in_dim(by_x, 0, cut, axis=other), 2)
        high = self.swap(lax.slice_in_dim(by_y, cut, 2 * cut, axis=other), 1)
        shape = list(block.shape)
        shape[axis] = size * 4
        out = jnp.zeros(shape, block.dtype)
        for part, bit, offset in ((block, 0, 0), (by_x, 1, 0), (by_y, 2, 0), (low, 3, 0), (high, 3, cut)):
            start = [0, 0]
            start[axis] = (self.place ^ bit) * size
            start[other] = offset
            out = lax.dynamic_update_slice(out, part, start)
        return out

    def scatter(self, partial, axis):
        if not self.square:
            total = lax.psum_scatter(partial, FSDP, scatter_dimension=axis, tiled=True)
            return total.astype(f32)
        other = 1 - axis
        size, cut = partial.shape[axis] // 4, partial.shape[other] // 2
        place = self.place

        def piece(bit, offset):
            start = [0, 0]
            start[axis] = (place ^ bit) * size
            start[other] = offset
            extent = [0, 0]
            extent[axis] = size
            extent[other] = cut
            return lax.dynamic_slice(partial, start, extent)

        halves = []
        for offset, first, second in ((0, 1, 2), (cut, 2, 1)):
            relay = self.swap(piece(3, offset), first)
            mine = self.swap(piece(first, offset), first)
            relay = (piece(second, offset).astype(f32) + relay.astype(f32)).astype(bf16)
            halves.append(
                piece(0, offset).astype(f32) + mine.astype(f32) + self.swap(relay, second).astype(f32)
            )
        return jnp.concatenate(halves, axis=other)

    def total(self, values):
        if not self.square:
            return lax.psum(values, FSDP)
        return values + self.swap(values, 1) + self.swap(values, 2) + self.swap(values, 3)

    def gather_small(self, values):
        if not self.square:
            return lax.all_gather(values, FSDP, axis=0, tiled=True)
        parts = [values] + [self.swap(values, bit) for bit in (1, 2, 3)]
        return jnp.concatenate(
            [
                lax.select_n(self.place ^ j, *parts)
                for j in range(4)
            ],
            axis=0,
        )


def per_device(
    tokens,
    positions,
    cotangent,
    w_attn,
    w_gate_up,
    w_down,
    gains,
    m_attn,
    v_attn,
    m_gate_up,
    v_gate_up,
    m_down,
    v_down,
    m_gains,
    v_gains,
):
    rows, width = tokens.shape
    owned = w_attn.shape[0]
    hidden = w_down.shape[1]
    count = lax.axis_size(FSDP)
    plane = Plane(count)
    place = plane.place
    length = rows * count
    part = width // count
    heads = part // HEAD_DIM
    wide = hidden // count
    scale = 1.0 / math.sqrt(HEAD_DIM)

    def spread(weight, groups, extra=None, tile=0):
        block = spread_kernel(weight, groups, count, extra, tile)
        return lax.all_to_all(block, FSDP, 0, 0, tiled=True)

    gain_block = jnp.pad(gains, ((0, 0), (0, GAIN_COLS - gains.shape[1])))
    attn_all = lax.all_gather(spread(w_attn, 4, gain_block), DP, axis=0, tiled=True)
    gate_up_all = lax.all_gather(spread(w_gate_up, 2, tile=TILE), DP, axis=0, tiled=True)
    down_all = lax.all_gather(spread(w_down, 1), DP, axis=0, tiled=True)
    qkv_weight = attn_all[:, : 3 * part]
    out_weight = attn_all[:, 3 * part : 4 * part]
    gain_values = attn_all[:, 4 * part : 4 * part + 4].astype(f32)
    gain_part = lax.dynamic_slice_in_dim(gain_values, place * part, part, 0)

    token_full = plane.gather(tokens, 0)
    position_full = plane.gather_small(positions)
    cot_part = lax.all_to_all(
        cotangent.reshape(rows, count, part).transpose(1, 0, 2).reshape(count * rows, part),
        FSDP,
        0,
        0,
        tiled=True,
    ).astype(f32)

    half_dim = HEAD_DIM // 2
    frequency = jnp.exp(
        jnp.arange(half_dim, dtype=f32) * (-2.0 * math.log(rope_base) / HEAD_DIM)
    )
    angles = position_full.astype(f32)[:, None] * frequency[None, :]
    cosine, sine = jnp.cos(angles), jnp.sin(angles)
    cosine = jnp.concatenate([cosine, cosine], axis=1)
    sine = jnp.concatenate([-sine, sine], axis=1)
    first_key = (jnp.arange(length, dtype=jnp.int32) - position_full)[:, None]
    gain_rows = jnp.pad(jnp.transpose(gain_part), ((0, 4), (0, 0)))
    attend, attend_back = attend_kernels(length, heads)

    qkv = mm(token_full, qkv_weight, ((1,), (0,)))
    query_raw, key_raw = qkv[:, :part], qkv[:, part : 2 * part]
    squares = plane.total(
        jnp.stack([jnp.sum(query_raw * query_raw, axis=1), jnp.sum(key_raw * key_raw, axis=1)])
    )
    inverse = jnp.transpose(lax.rsqrt(squares / width + norm_eps))
    tables = (inverse, gain_rows, cosine, sine, first_key)
    query, key, value, attended_low, lse = attend(qkv, *tables)
    attended_full = plane.gather(attended_low, 1)

    branch = mm(attended_full, out_weight, ((1,), (0,)))
    branch_inv = lax.rsqrt(plane.total(jnp.sum(branch * branch, axis=1)) / width + norm_eps)[:, None]
    branch_hat = branch * branch_inv
    token_part = lax.dynamic_slice_in_dim(token_full, place * part, part, 1).astype(f32)
    hidden_low = (token_part + branch_hat * gain_part[None, :, 2]).astype(bf16)
    hidden_full = plane.gather(hidden_low, 1)

    copies, core = lax.axis_size("z"), lax.axis_index("core")
    share = width // (2 * copies)

    def side(index):
        return jnp.concatenate(
            [
                lax.dynamic_slice_in_dim(hidden_full, (2 * z + index) * share, share, 1)
                for z in range(copies)
            ],
            axis=1,
        )

    other_side, own_side = side(1 - core), side(core)
    hidden_full = order(order(hidden_full, other_side), own_side)
    gate_up, gate_up_back = gate_up_kernels(length, width, wide)
    both, activ = gate_up(hidden_full, gate_up_all)
    mlp = plane.scatter(mm(activ, down_all, ((1,), (1,))).astype(bf16), 0)
    mlp_inv = lax.rsqrt(jnp.mean(mlp * mlp, axis=1, keepdims=True) + norm_eps)
    mlp_hat = mlp * mlp_inv
    hidden_rows = lax.dynamic_slice_in_dim(hidden_full, place * rows, rows, 0).astype(f32)
    output = (hidden_rows + mlp_hat * gain_values[None, :, 3]).astype(bf16)

    grad_out = cotangent.astype(f32)
    scaled = grad_out * gain_values[None, :, 3]
    grad_mlp = mlp_inv * (scaled - mlp_hat * jnp.mean(scaled * mlp_hat, axis=1, keepdims=True))
    grad_gain_mlp = jnp.sum(grad_out * mlp_hat, axis=0)
    grad_mlp_full = with_layout_constraint(
        plane.gather(grad_mlp.astype(bf16), 0), Layout(major_to_minor=(0, 1))
    )

    def reduced(partial, axes, wait=()):
        mine = lax.psum_scatter(partial, axes, scatter_dimension=0, tiled=True)
        for other in wait:
            mine = order(mine, other)
        return mine, lax.all_to_all(mine, FSDP, 0, 0, tiled=True)

    down_mine, down_part = reduced(mm(grad_mlp_full, activ, ((0,), (0,))).astype(bf16), DP)
    grad_gate_up_low = gate_up_back(grad_mlp_full, down_all, both)

    send = mm(other_side, grad_gate_up_low, ((0,), (0,))).astype(bf16)
    got = lax.ppermute(send, "core", [(0, 1), (1, 0)])
    late = order(grad_gate_up_low, send)
    keep = mm(own_side, late, ((0,), (0,))).astype(bf16)
    late = order(late, keep)
    grad_hidden = cot_part + plane.scatter(
        mm(late, gate_up_all, ((1,), (1,))).astype(bf16), 1
    )
    gate_up_partial = (keep.astype(f32) + got.astype(f32)).astype(bf16)
    gate_up_mine, gate_up_part = reduced(gate_up_partial, "z")

    scaled = grad_hidden * gain_part[None, :, 2]
    grad_gain_attn = jnp.sum(grad_hidden * branch_hat, axis=0)
    inner = plane.total(jnp.sum(scaled * branch_hat, axis=1))[:, None] / width
    grad_branch = (branch_inv * (scaled - branch_hat * inner)).astype(bf16)
    grad_branch = order(grad_branch, down_mine)
    grad_att = plane.scatter(mm(grad_branch, out_weight, ((1,), (1,))).astype(bf16), 1)
    query_grad, key_grad, value_grad, gain_grad, inner = attend_back(
        query, key, value, attended_low, grad_att, lse, qkv, *tables
    )
    inner = jnp.transpose(plane.total(jnp.transpose(inner[:, :2])) / width)
    grad_qkv_low = qkv_back(query_grad, key_grad, value_grad, qkv, inverse, inner)

    own_gains = jnp.concatenate([gain_grad[:2], grad_gain_attn[None], jnp.zeros((5, part), f32)])
    gain_rows = jnp.pad(grad_gain_mlp[None], ((3, 4), (0, 0)))
    gain_rows = lax.dynamic_update_slice(
        gain_rows,
        own_gains + lax.dynamic_slice_in_dim(gain_rows, place * part, part, 1),
        (0, place * part),
    )
    lefts = (jnp.transpose(token_full), grad_qkv_low, jnp.transpose(attended_full), grad_branch)
    attn_partial = attn_grad(*lefts, gain_rows)
    attn_partial = order(attn_partial, gate_up_mine)
    back = token_grad(
        jnp.full((1,), place), order(grad_qkv_low, attn_partial), attn_all, grad_hidden
    )
    grad_down, new_down, new_m_down, new_v_down = adamw_kernel(
        down_part, w_down, m_down, v_down, 1, count
    )
    grad_gate_up, new_gate_up, new_m_gate_up, new_v_gate_up = adamw_kernel(
        gate_up_part, w_gate_up, m_gate_up, v_gate_up, 2, count, TILE
    )
    _, attn_part = reduced(attn_partial, DP, (new_down, new_gate_up))
    grad_gains = jnp.sum(
        attn_part[:, 4 * part : 4 * part + 4].reshape(count, owned, 4).astype(f32), axis=0
    )

    grad_tokens = plane.scatter(back, 0)
    grad_attn, new_attn, new_m_attn, new_v_attn = adamw_kernel(
        attn_part, w_attn, m_attn, v_attn, 4, count
    )
    new_gains, new_m_gains, new_v_gains = adamw_step(
        gains, grad_gains, m_gains, v_gains, 0.0, gain_rate
    )
    return (
        output,
        grad_tokens,
        grad_attn,
        grad_gate_up,
        grad_down,
        grad_gains,
        new_attn,
        new_gate_up,
        new_down,
        new_gains,
        new_m_attn,
        new_v_attn,
        new_m_gate_up,
        new_v_gate_up,
        new_m_down,
        new_v_down,
        new_m_gains,
        new_v_gains,
    )


def solution(mesh):
    copies, places = mesh.devices.shape
    mesh = Mesh(mesh.devices.reshape(copies // 2, 2, 2, places // 2), DP + FSDP)
    matrix, vector = P(DP + FSDP, None), P(DP + FSDP)
    in_specs = (matrix, vector) + (matrix,) * 13
    return jax.shard_map(
        per_device, mesh=mesh, in_specs=in_specs, out_specs=(matrix,) * 18, check_vma=False
    )
```

```python
import functools
import math

import jax
import jax.numpy as jnp
from jax import lax
from jax.experimental import pallas as pl
from jax.experimental.pallas import tpu as pltpu
from jax.experimental.layout import Layout, with_layout_constraint
from jax.sharding import Mesh
from jax.sharding import PartitionSpec as P

HEAD_DIM = 128

norm_eps = 1e-06
rope_base = 500000.0
learn_rate = 0.004
gain_rate = 0.25
beta_one = 0.9
beta_two = 0.95
decay_rate = 0.1
adam_eps = 1e-08
correct_one = 1.0 - beta_one**2
correct_two = 1.0 - beta_two**2
neg_large = -1e30
bf16 = jnp.bfloat16
f32 = jnp.float32
TILE = 512
ALL_VMEM = 60 * 1024 * 1024


def mm(left, right, dims):
    return lax.dot_general(left, right, (dims, ((), ())), preferred_element_type=f32)


def adamw_step(weight, gradient, moment, second, decay_coef, rate_value):
    moment_new = beta_one * moment + (1.0 - beta_one) * gradient
    second_new = beta_two * second + (1.0 - beta_two) * gradient * gradient
    step_ratio = moment_new / correct_one / (jnp.sqrt(second_new / correct_two) + adam_eps)
    return (
        weight * (1.0 - rate_value * decay_coef) - rate_value * step_ratio,
        moment_new,
        second_new,
    )


def spread_body(tile, *refs):
    out = refs[-1]
    if tile:
        for i in range(refs[0].shape[1] // tile):
            for g, ref in enumerate(refs[:-1]):
                start = (i * len(refs[:-1]) + g) * tile
                out[:, start : start + tile] = ref[:, i * tile : (i + 1) * tile].astype(bf16)
        return
    start = 0
    for ref in refs[:-1]:
        out[:, start : start + ref.shape[1]] = ref[...].astype(bf16)
        start += ref.shape[1]


def spread_kernel(weight, groups, count, tile):
    owned, columns = weight.shape
    size = columns // (groups * count)
    specs = [
        pl.BlockSpec((owned, size), lambda f, g=g: (0, g * count + f)) for g in range(groups)
    ]
    operands = [weight] * groups
    wide = groups * size
    return pl.pallas_call(
        functools.partial(spread_body, tile),
        grid=(count,),
        in_specs=specs,
        out_specs=pl.BlockSpec((owned, wide), lambda f: (f, 0)),
        out_shape=jax.ShapeDtypeStruct((count * owned, wide), bf16),
        compiler_params=pltpu.CompilerParams(vmem_limit_bytes=40 * 1024 * 1024),
        cost_estimate=pl.CostEstimate(
            flops=0, bytes_accessed=6 * owned * columns, transcendentals=0
        ),
    )(*operands)


def adamw_body(tile, *refs):
    grad_in, weight, moment, second, grad_out, new_weight, new_moment, new_second = refs
    if tile:
        groups = grad_in.shape[1] // weight.shape[1]
        for i in range(weight.shape[1] // tile):
            start = pl.multiple_of((i * groups + pl.program_id(1)) * tile, tile)
            grad_out[:, i * tile : (i + 1) * tile] = grad_in[:, pl.ds(start, tile)].astype(f32)
    else:
        grad_out[...] = grad_in[...].astype(f32)
    new_weight[...], new_moment[...], new_second[...] = adamw_step(
        weight[...], grad_out[...], moment[...], second[...], decay_rate, learn_rate
    )


def adamw_kernel(gradient, weight, moment, second, groups, count, tile=0):
    owned, columns = weight.shape
    size = columns // (groups * count)
    whole = pl.BlockSpec((owned, size), lambda f, g: (0, g * count + f))
    if tile:
        grad_spec = pl.BlockSpec((owned, groups * size), lambda f, g: (f, 0))
    else:
        grad_spec = pl.BlockSpec((owned, size), lambda f, g: (f, g))
    return pl.pallas_call(
        functools.partial(adamw_body, tile),
        grid=(count, groups),
        in_specs=[grad_spec, whole, whole, whole],
        out_specs=[whole] * 4,
        out_shape=[jax.ShapeDtypeStruct(weight.shape, f32)] * 4,
        compiler_params=pltpu.CompilerParams(vmem_limit_bytes=40 * 1024 * 1024),
        cost_estimate=pl.CostEstimate(
            flops=12 * owned * columns, bytes_accessed=30 * owned * columns, transcendentals=0
        ),
    )(gradient, weight, moment, second)


def dot(left, right, left_dim, right_dim):
    return lax.dot_general(
        left, right, (((left_dim,), (right_dim,)), ((), ())), preferred_element_type=f32
    )


def visible(first_ref, low, high):
    shape = (high - low, high)
    row = lax.broadcasted_iota(jnp.int32, shape, 0) + low
    column = lax.broadcasted_iota(jnp.int32, shape, 1)
    return (column <= row) & (column >= first_ref[low:high, :])


def attend_body(block, scale, *refs):
    query_in, key_in, value_in, inverse, gain, cosine, sine, first = refs[:8]
    query_out, key_out, value_out, attended, lse = refs[8:]

    def turned(values, column):
        normed = values * inverse[:, column : column + 1] * gain[column : column + 1, :]
        return (normed * cosine[...] + pltpu.roll(normed, HEAD_DIM // 2, 1) * sine[...]).astype(bf16)

    query_out[...] = turned(query_in[...], 0)
    key_out[...] = turned(key_in[...], 1)
    value_out[...] = value_in[...].astype(bf16)
    for low in range(0, query_in.shape[0], block):
        high = low + block
        scores = dot(query_out[low:high, :], key_out[:high, :], 1, 1) * scale
        scores = jnp.where(visible(first, low, high), scores, neg_large)
        top = jnp.max(scores, axis=1, keepdims=True)
        weights = jnp.exp(scores - top)
        denom = jnp.sum(weights, axis=1, keepdims=True)
        attended[low:high, :] = (
            dot(weights.astype(bf16), value_out[:high, :], 1, 0) / denom
        ).astype(bf16)
        lse[0, low:high, :] = top + jnp.log(denom)


def attend_back_body(block, scale, *refs):
    query, key, value, attended, grad_att, lse = refs[:6]
    query_in, key_in, inverse, gain, cosine, sine, first = refs[6:13]
    query_grad, key_grad, value_grad, gain_grad, inner = refs[13:18]
    key_sum, value_sum = refs[18:]
    grad_low = grad_att
    delta = jnp.sum(
        grad_low[...].astype(f32) * attended[...].astype(f32), axis=1, keepdims=True
    )
    key_sum[...] = jnp.zeros_like(key_sum)
    value_sum[...] = jnp.zeros_like(value_sum)
    for low in range(0, query.shape[0], block):
        high = low + block
        scores = dot(query[low:high, :], key[:high, :], 1, 1) * scale
        prob = jnp.where(
            visible(first, low, high), jnp.exp(scores - lse[0, low:high, :]), 0.0
        )
        grad_prob = dot(grad_low[low:high, :], value[:high, :], 1, 1)
        grad_scores = (prob * (grad_prob - delta[low:high, :])).astype(bf16)
        query_grad[low:high, :] = dot(grad_scores, key[:high, :], 1, 0) * scale
        key_sum[:high, :] += dot(grad_scores, query[low:high, :], 0, 0)
        value_sum[:high, :] += dot(prob.astype(bf16), grad_low[low:high, :], 0, 0)
    value_grad[...] = value_sum[...].astype(bf16)
    lane = lax.broadcasted_iota(jnp.int32, inner.shape, 1)

    @pl.when(pl.program_id(0) == 0)
    def _():
        inner[...] = jnp.zeros_like(inner)

    gain_grad[...] = jnp.zeros_like(gain_grad)
    for column, turned, raw, out in (
        (0, query_grad[...], query_in, query_grad),
        (1, key_sum[...] * scale, key_in, key_grad),
    ):
        back = turned * cosine[...] - pltpu.roll(turned, HEAD_DIM // 2, 1) * sine[...]
        hat = raw[...] * inverse[:, column : column + 1]
        gain_grad[column : column + 1, :] = jnp.sum(back * hat, axis=0, keepdims=True)
        back = back * gain[column : column + 1, :]
        out[...] = back
        inner[...] += jnp.where(
            lane == column, jnp.sum(back * hat, axis=1, keepdims=True), 0.0
        )


def attend_kernels(length, heads):
    block = math.gcd(length, 256)
    scale = 1.0 / math.sqrt(HEAD_DIM)
    part = heads * HEAD_DIM

    def own(shift=0):
        return pl.BlockSpec((length, HEAD_DIM), lambda h: (0, h + shift))

    def same(width):
        return pl.BlockSpec((length, width), lambda h: (0, 0))

    gain_spec = pl.BlockSpec((8, HEAD_DIM), lambda h: (0, h))
    lse_spec = pl.BlockSpec((1, length, 1), lambda h: (h, 0, 0))
    tables = [same(2), gain_spec, same(HEAD_DIM), same(HEAD_DIM), same(1)]
    low_shape = jax.ShapeDtypeStruct((length, part), bf16)
    wide_shape = jax.ShapeDtypeStruct((length, part), f32)
    work = 2 * heads * length * length * HEAD_DIM
    params = pltpu.CompilerParams(vmem_limit_bytes=48 * 1024 * 1024)

    def forward(qkv, *rest):
        return pl.pallas_call(
            functools.partial(attend_body, block, scale),
            grid=(heads,),
            in_specs=[own(), own(heads), own(2 * heads)] + tables,
            out_specs=[own()] * 4 + [lse_spec],
            out_shape=[low_shape] * 4 + [jax.ShapeDtypeStruct((heads, length, 1), f32)],
            compiler_params=params,
            cost_estimate=pl.CostEstimate(
                flops=2 * work, bytes_accessed=20 * length * part, transcendentals=0
            ),
        )(qkv, qkv, qkv, *rest)

    def backward(query, key, value, attended, grad_att, lse, qkv, *rest):
        return pl.pallas_call(
            functools.partial(attend_back_body, block, scale),
            grid=(heads,),
            in_specs=[own()] * 5 + [lse_spec, own(), own(heads)] + tables,
            out_specs=[own()] * 3 + [gain_spec, same(HEAD_DIM)],
            out_shape=[
                wide_shape,
                wide_shape,
                low_shape,
                jax.ShapeDtypeStruct((8, part), f32),
                jax.ShapeDtypeStruct((length, HEAD_DIM), f32),
            ],
            scratch_shapes=[
                pltpu.VMEM((length, HEAD_DIM), f32),
                pltpu.VMEM((length, HEAD_DIM), f32),
            ],
            compiler_params=params,
            cost_estimate=pl.CostEstimate(
                flops=5 * work, bytes_accessed=30 * length * part, transcendentals=0
            ),
        )(query, key, value, attended, grad_att, lse, qkv, qkv, *rest)

    return forward, backward


def qkv_back_body(query_grad, key_grad, value_grad, raw, inverse, inner, out):
    part = query_grad.shape[1]
    for column, grad in ((0, query_grad), (1, key_grad)):
        scale = inverse[:, column : column + 1]
        hat = raw[:, column * part : (column + 1) * part] * scale
        out[:, column * part : (column + 1) * part] = (
            scale * (grad[...] - hat * inner[:, column : column + 1])
        ).astype(bf16)
    out[:, 2 * part :] = value_grad[...]


def qkv_back(query_grad, key_grad, value_grad, qkv, inverse, inner):
    length, part = query_grad.shape
    rows = math.gcd(length, 256)

    def spec(width):
        return pl.BlockSpec((rows, width), lambda i: (i, 0))

    return pl.pallas_call(
        qkv_back_body,
        grid=(length // rows,),
        in_specs=[spec(part)] * 3 + [spec(2 * part), spec(2), spec(2)],
        out_specs=spec(3 * part),
        out_shape=jax.ShapeDtypeStruct((length, 3 * part), bf16),
        compiler_params=pltpu.CompilerParams(vmem_limit_bytes=ALL_VMEM),
        cost_estimate=pl.CostEstimate(
            flops=8 * length * part, bytes_accessed=24 * length * part, transcendentals=0
        ),
    )(query_grad, key_grad, value_grad, qkv, inverse, inner)


def attn_grad_body(token, grad_qkv, attended, grad_branch, *rest):
    out = rest[-1]
    wide = grad_qkv.shape[1]
    for low, high, left, right in (
        (0, wide, token, grad_qkv),
        (wide, out.shape[1], attended, grad_branch),
    ):
        value = dot(left[...], right[...], 1, 0)
        if len(rest) > 1:
            value = value + rest[0][:, low:high].astype(f32)
        out[:, low:high] = value.astype(bf16)


def attn_grad(token, grad_qkv, attended, grad_branch, *other):
    width, length = token.shape
    rows = math.gcd(width, 512)
    columns = grad_qkv.shape[1] + grad_branch.shape[1]

    def row_spec(wide):
        return pl.BlockSpec((rows, wide), lambda i: (i, 0))

    def whole(array):
        return pl.BlockSpec(array.shape, lambda i: (0, 0))

    return pl.pallas_call(
        attn_grad_body,
        grid=(width // rows,),
        in_specs=[row_spec(length), whole(grad_qkv), row_spec(length), whole(grad_branch)]
        + [row_spec(columns)] * len(other),
        out_specs=row_spec(columns),
        out_shape=jax.ShapeDtypeStruct((width, columns), bf16),
        compiler_params=pltpu.CompilerParams(vmem_limit_bytes=48 * 1024 * 1024),
        cost_estimate=pl.CostEstimate(
            flops=2 * width * length * columns,
            bytes_accessed=6 * width * length,
            transcendentals=0,
        ),
    )(token, grad_qkv, attended, grad_branch, *other)


def token_grad_body(place, grad_qkv, weight, grad_hidden, out):
    own = (pl.program_id(0) == place[0]).astype(f32)
    out[...] = (dot(grad_qkv[...], weight[...], 1, 1) + own * grad_hidden[...]).astype(bf16)


def token_grad(place, grad_qkv, weight, grad_hidden):
    length, wide = grad_qkv.shape
    width, part = weight.shape[0], grad_hidden.shape[1]
    return pl.pallas_call(
        token_grad_body,
        grid_spec=pltpu.PrefetchScalarGridSpec(
            num_scalar_prefetch=1,
            grid=(width // part,),
            in_specs=[
                pl.BlockSpec((length, wide), lambda j, place: (0, 0)),
                pl.BlockSpec((part, wide), lambda j, place: (j, 0)),
                pl.BlockSpec((length, part), lambda j, place: (0, 0)),
            ],
            out_specs=pl.BlockSpec((length, part), lambda j, place: (0, j)),
        ),
        out_shape=jax.ShapeDtypeStruct((length, width), bf16),
        compiler_params=pltpu.CompilerParams(vmem_limit_bytes=48 * 1024 * 1024),
        cost_estimate=pl.CostEstimate(
            flops=2 * width * length * wide, bytes_accessed=8 * width * length, transcendentals=0
        ),
    )(place, grad_qkv, weight, grad_hidden)


def half_grad_body(left, right, *rest):
    value = dot(left[...], right[...], 1, 0)
    if len(rest) > 1:
        value = value + rest[0][...].astype(f32)
    rest[-1][...] = value.astype(bf16)


def half_grad(left, right, *other):
    rows, length = left.shape
    columns = right.shape[1]
    size = math.gcd(columns, 512)
    spec = pl.BlockSpec((rows, size), lambda j: (0, j))
    return pl.pallas_call(
        half_grad_body,
        grid=(columns // size,),
        in_specs=[
            pl.BlockSpec((rows, length), lambda j: (0, 0)),
            pl.BlockSpec((length, size), lambda j: (0, j)),
        ]
        + [spec] * len(other),
        out_specs=spec,
        out_shape=jax.ShapeDtypeStruct((rows, columns), bf16),
        compiler_params=pltpu.CompilerParams(vmem_limit_bytes=48 * 1024 * 1024),
        cost_estimate=pl.CostEstimate(
            flops=2 * rows * length * columns, bytes_accessed=4 * rows * columns, transcendentals=0
        ),
    )(left, right, *other)


def gate_up_body(hidden, weight, both, activ):
    value = dot(hidden[...], weight[...], 1, 0)
    gate, up = value[:, :TILE], value[:, TILE:]
    sigmoid = jax.nn.sigmoid(gate)
    silu = gate * sigmoid
    activ[...] = (silu * up).astype(bf16)
    both[:, :TILE] = up * sigmoid * (1.0 + gate * (1.0 - sigmoid))
    both[:, TILE:] = silu


def gate_up_back_body(grad_mlp, weight, both, out):
    grad = dot(grad_mlp[...], weight[...], 1, 0)
    for start in (0, TILE):
        out[:, start : start + TILE] = (grad * both[:, start : start + TILE]).astype(bf16)


def gate_up_kernels(length, width, wide):
    params = pltpu.CompilerParams(vmem_limit_bytes=48 * 1024 * 1024)
    rows_spec = pl.BlockSpec((length, width), lambda j: (0, 0))

    def columns(rows, size):
        return pl.BlockSpec((rows, size), lambda j: (0, j))

    def forward(hidden, weight):
        return pl.pallas_call(
            gate_up_body,
            grid=(wide // TILE,),
            in_specs=[rows_spec, columns(width, 2 * TILE)],
            out_specs=[columns(length, 2 * TILE), columns(length, TILE)],
            out_shape=[
                jax.ShapeDtypeStruct((length, 2 * wide), f32),
                jax.ShapeDtypeStruct((length, wide), bf16),
            ],
            compiler_params=params,
            cost_estimate=pl.CostEstimate(
                flops=4 * length * width * wide,
                bytes_accessed=10 * length * wide + 4 * width * wide,
                transcendentals=0,
            ),
        )(hidden, weight)

    def backward(grad_mlp, weight, both):
        return pl.pallas_call(
            gate_up_back_body,
            grid=(wide // TILE,),
            in_specs=[rows_spec, columns(width, TILE), columns(length, 2 * TILE)],
            out_specs=columns(length, 2 * TILE),
            out_shape=jax.ShapeDtypeStruct((length, 2 * wide), bf16),
            compiler_params=pltpu.CompilerParams(vmem_limit_bytes=ALL_VMEM),
            cost_estimate=pl.CostEstimate(
                flops=2 * length * width * wide,
                bytes_accessed=12 * length * wide + 2 * width * wide,
                transcendentals=0,
            ),
        )(grad_mlp, weight, both)

    return forward, backward


FSDP, DP = ("y", "x"), ("z", "core")


def order_body(values, other, out):
    pass


def order(values, other):
    anywhere = pl.BlockSpec(memory_space=pl.ANY)
    return pl.pallas_call(
        order_body,
        in_specs=[anywhere, anywhere],
        out_specs=anywhere,
        out_shape=jax.ShapeDtypeStruct(values.shape, values.dtype),
        input_output_aliases={0: 0},
    )(values, other)


def zero_after(other):
    first = other[(slice(0, 1),) * other.ndim].astype(f32).reshape(())
    return jnp.minimum(jnp.abs(first), 0.0).astype(jnp.int32)


class Copies:
    def __init__(self):
        self.count = lax.axis_size("z")

    def swap(self, values):
        return lax.ppermute(values, "core", [(0, 1), (1, 0)])

    def along(self, values):
        return [values] + [
            lax.ppermute(values, "z", [(i, (i + step) % self.count) for i in range(self.count)])
            for step in range(1, self.count)
        ]

    def gather(self, values):
        core, place = lax.axis_index("core"), lax.axis_index("z")
        other = self.swap(values)
        both = jnp.concatenate(
            [lax.select_n(core, values, other), lax.select_n(core, other, values)]
        )
        parts = self.along(both)
        return jnp.concatenate(
            [lax.select_n((place - z) % self.count, *parts) for z in range(self.count)]
        )

    def total(self, values):
        return sum(self.along(values + self.swap(values)))


class Plane:
    def __init__(self, count):
        self.count = count
        self.square = count == 4
        self.place = lax.axis_index(FSDP)

    def swap(self, values, bit):
        return lax.ppermute(values, FSDP, [(i, i ^ bit) for i in range(self.count)])

    def gather(self, block, axis):
        if not self.square:
            return lax.all_gather(block, FSDP, axis=axis, tiled=True)
        other = 1 - axis
        size, cut = block.shape[axis], block.shape[other] // 2
        by_x, by_y = self.swap(block, 1), self.swap(block, 2)
        low = self.swap(lax.slice_in_dim(by_x, 0, cut, axis=other), 2)
        high = self.swap(lax.slice_in_dim(by_y, cut, 2 * cut, axis=other), 1)
        shape = list(block.shape)
        shape[axis] = size * 4
        out = jnp.zeros(shape, block.dtype)
        for part, bit, offset in ((block, 0, 0), (by_x, 1, 0), (by_y, 2, 0), (low, 3, 0), (high, 3, cut)):
            start = [0, 0]
            start[axis] = (self.place ^ bit) * size
            start[other] = offset
            out = lax.dynamic_update_slice(out, part, start)
        return out

    def scatter(self, partial, axis, kind=f32, last=(0, 0)):
        if not self.square:
            total = lax.psum_scatter(partial, FSDP, scatter_dimension=axis, tiled=True)
            return total.astype(f32)
        other = 1 - axis
        size, cut = partial.shape[axis] // 4, partial.shape[other] // 2
        place = self.place

        def piece(bit, offset, zero=0):
            start = [0, 0]
            start[axis] = (place ^ bit) * size + zero
            start[other] = offset
            extent = [0, 0]
            extent[axis] = size
            extent[other] = cut
            return lax.dynamic_slice(partial, start, extent)

        halves = []
        for (offset, first, second), zero in zip(((0, 1, 2), (cut, 2, 1)), last):
            relay = self.swap(piece(3, offset), first)
            mine = self.swap(piece(first, offset), first)
            relay = (piece(second, offset).astype(f32) + relay.astype(f32)).astype(bf16)
            halves.append(
                piece(0, offset, zero).astype(f32) + mine.astype(f32) + self.swap(relay, second).astype(f32)
            )
        return jnp.concatenate([half.astype(kind) for half in halves], axis=other)

    def total(self, values):
        if not self.square:
            return lax.psum(values, FSDP)
        return values + self.swap(values, 1) + self.swap(values, 2) + self.swap(values, 3)

    def gather_small(self, values):
        if not self.square:
            return lax.all_gather(values, FSDP, axis=0, tiled=True)
        parts = [values] + [self.swap(values, bit) for bit in (1, 2, 3)]
        return jnp.concatenate(
            [
                lax.select_n(self.place ^ j, *parts)
                for j in range(4)
            ],
            axis=0,
        )


def per_device(
    tokens,
    positions,
    cotangent,
    w_attn,
    w_gate_up,
    w_down,
    gains,
    m_attn,
    v_attn,
    m_gate_up,
    v_gate_up,
    m_down,
    v_down,
    m_gains,
    v_gains,
):
    rows, width = tokens.shape
    owned = w_attn.shape[0]
    hidden = w_down.shape[1]
    count = lax.axis_size(FSDP)
    plane = Plane(count)
    place = plane.place
    length = rows * count
    part = width // count
    heads = part // HEAD_DIM
    wide = hidden // count
    scale = 1.0 / math.sqrt(HEAD_DIM)

    def spread(weight, groups, tile=0):
        block = spread_kernel(weight, groups, count, tile)
        return lax.all_to_all(block, FSDP, 0, 0, tiled=True)

    attn_all = lax.all_gather(spread(w_attn, 4), DP, axis=0, tiled=True)
    gate_up_all = lax.all_gather(spread(w_gate_up, 2, tile=TILE), DP, axis=0, tiled=True)
    down_all = lax.all_gather(spread(w_down, 1), DP, axis=0, tiled=True)
    qkv_weight = attn_all[:, : 3 * part]
    out_weight = attn_all[:, 3 * part : 4 * part]
    copies = Copies()
    gain_low = lax.reduce_precision(gains, exponent_bits=8, mantissa_bits=7)
    gain_values = copies.gather(plane.gather_small(jnp.transpose(gain_low).reshape(-1)))
    gain_values = jnp.transpose(gain_values.reshape(-1, 4, owned), (0, 2, 1)).reshape(width, 4)
    gain_part = lax.dynamic_slice_in_dim(gain_values, place * part, part, 0)

    token_full = plane.gather(tokens, 0)
    position_full = plane.gather_small(positions)
    cot_part = lax.all_to_all(
        cotangent.reshape(rows, count, part).transpose(1, 0, 2).reshape(count * rows, part),
        FSDP,
        0,
        0,
        tiled=True,
    ).astype(f32)

    half_dim = HEAD_DIM // 2
    frequency = jnp.exp(
        jnp.arange(half_dim, dtype=f32) * (-2.0 * math.log(rope_base) / HEAD_DIM)
    )
    angles = position_full.astype(f32)[:, None] * frequency[None, :]
    cosine, sine = jnp.cos(angles), jnp.sin(angles)
    cosine = jnp.concatenate([cosine, cosine], axis=1)
    sine = jnp.concatenate([-sine, sine], axis=1)
    first_key = (jnp.arange(length, dtype=jnp.int32) - position_full)[:, None]
    gain_rows = jnp.pad(jnp.transpose(gain_part), ((0, 4), (0, 0)))
    attend, attend_back = attend_kernels(length, heads)

    qkv = mm(token_full, qkv_weight, ((1,), (0,)))
    query_raw, key_raw = qkv[:, :part], qkv[:, part : 2 * part]
    squares = plane.total(
        jnp.concatenate([jnp.sum(query_raw * query_raw, axis=1), jnp.sum(key_raw * key_raw, axis=1)])
    )
    inverse = jnp.transpose(lax.rsqrt(squares / width + norm_eps).reshape(2, length))
    tables = (inverse, gain_rows, cosine, sine, first_key)
    query, key, value, attended_low, lse = attend(qkv, *tables)
    attended_full = plane.gather(attended_low, 1)

    branch = mm(attended_full, out_weight, ((1,), (0,)))
    branch_inv = lax.rsqrt(plane.total(jnp.sum(branch * branch, axis=1)) / width + norm_eps)[:, None]
    branch_hat = branch * branch_inv
    token_part = lax.dynamic_slice_in_dim(token_full, place * part, part, 1).astype(f32)
    hidden_low = (token_part + branch_hat * gain_part[None, :, 2]).astype(bf16)
    hidden_full = plane.gather(hidden_low, 1)

    core = lax.axis_index("core")
    share = width // (2 * copies.count)

    def sides(array):
        return [
            jnp.transpose(
                jnp.concatenate(
                    [
                        lax.dynamic_slice_in_dim(array, (2 * z + index) * share, share, 1)
                        for z in range(copies.count)
                    ],
                    axis=1,
                )
            )
            for index in (1 - core, core)
        ]

    other_side, own_side = sides(hidden_full)
    token_turned, attended_turned = jnp.transpose(token_full), jnp.transpose(attended_full)
    for early in (other_side, own_side, token_turned, attended_turned, cot_part):
        hidden_full = order(hidden_full, early)
    gate_up, gate_up_back = gate_up_kernels(length, width, wide)
    both, activ = gate_up(hidden_full, gate_up_all)
    mlp = plane.scatter(mm(activ, down_all, ((1,), (1,))).astype(bf16), 0)
    mlp_inv = lax.rsqrt(jnp.mean(mlp * mlp, axis=1, keepdims=True) + norm_eps)
    mlp_hat = mlp * mlp_inv
    hidden_rows = lax.dynamic_slice_in_dim(hidden_full, place * rows, rows, 0).astype(f32)
    output = (hidden_rows + mlp_hat * gain_values[None, :, 3]).astype(bf16)

    grad_out = cotangent.astype(f32)
    scaled = grad_out * gain_values[None, :, 3]
    grad_mlp = mlp_inv * (scaled - mlp_hat * jnp.mean(scaled * mlp_hat, axis=1, keepdims=True))
    grad_gain_mlp = jnp.sum(grad_out * mlp_hat, axis=0)
    grad_mlp_full = with_layout_constraint(
        plane.gather(grad_mlp.astype(bf16), 0), Layout(major_to_minor=(0, 1))
    )

    def exchanged(mine, *wait):
        for other in wait:
            mine = order(mine, other)
        return lax.all_to_all(mine, FSDP, 0, 0, tiled=True)

    down_partial = mm(grad_mlp_full, activ, ((0,), (0,))).astype(bf16)
    down_mine = lax.psum_scatter(down_partial, DP, scatter_dimension=0, tiled=True)
    grad_gate_up_low = gate_up_back(grad_mlp_full, down_all, both)

    send = half_grad(other_side, grad_gate_up_low)
    got = copies.swap(send)
    late = order(grad_gate_up_low, send)
    hidden_partial = mm(late, gate_up_all, ((1,), (1,))).astype(bf16)
    grad_hidden = cot_part + plane.scatter(hidden_partial, 1)
    gate_up_partial = half_grad(order(own_side, hidden_partial), late, got)
    gate_up_mine = lax.psum_scatter(gate_up_partial, "z", scatter_dimension=0, tiled=True)

    scaled = grad_hidden * gain_part[None, :, 2]
    grad_gain_attn = jnp.sum(grad_hidden * branch_hat, axis=0)
    inner = plane.total(jnp.sum(scaled * branch_hat, axis=1))[:, None] / width
    grad_branch = (branch_inv * (scaled - branch_hat * inner)).astype(bf16)
    grad_branch = order(grad_branch, down_mine)
    grad_att = plane.scatter(
        mm(grad_branch, out_weight, ((1,), (1,))).astype(bf16), 1, bf16
    )
    query_grad, key_grad, value_grad, gain_grad, inner = attend_back(
        query, key, value, attended_low, grad_att, lse, qkv, *tables
    )
    inner = plane.total(jnp.concatenate([inner[:, 0], inner[:, 1]])) / width
    inner = jnp.transpose(inner.reshape(2, length))
    grad_qkv_low = qkv_back(query_grad, key_grad, value_grad, qkv, inverse, inner)

    own_gains = jnp.stack([gain_grad[0], gain_grad[1], grad_gain_attn])
    gain_sums = jnp.concatenate([jnp.zeros((3, width), f32), grad_gain_mlp[None]])
    gain_sums = lax.dynamic_update_slice(gain_sums, own_gains, (0, place * part)).reshape(-1)
    gain_sums = plane.total(copies.total(gain_sums)).reshape(4, width)
    owner = lax.axis_index(DP + FSDP)
    grad_gains = jnp.transpose(lax.dynamic_slice_in_dim(gain_sums, owner * owned, owned, 1))
    attn_partial = attn_grad(token_turned, grad_qkv_low, attended_turned, grad_branch)
    late = order(grad_qkv_low, attn_partial)
    back = token_grad(jnp.full((1,), place), late, attn_all, grad_hidden)
    attn_partial = order(order(attn_partial, back), gate_up_mine)
    attn_mine = lax.psum_scatter(attn_partial, DP, scatter_dimension=0, tiled=True)
    gate_up_part = exchanged(gate_up_mine, attn_partial)
    grad_tokens = plane.scatter(
        back, 0, last=(zero_after(gate_up_part), zero_after(grad_gains))
    )
    grad_down, new_down, new_m_down, new_v_down = adamw_kernel(
        exchanged(down_mine, attn_partial), w_down, m_down, v_down, 1, count
    )
    attn_mine = order(order(attn_mine, grad_tokens), new_down)
    attn_part = exchanged(attn_mine)
    grad_gate_up, new_gate_up, new_m_gate_up, new_v_gate_up = adamw_kernel(
        order(gate_up_part, attn_mine), w_gate_up, m_gate_up, v_gate_up, 2, count, TILE
    )
    grad_attn, new_attn, new_m_attn, new_v_attn = adamw_kernel(
        order(attn_part, new_gate_up), w_attn, m_attn, v_attn, 4, count
    )
    new_gains, new_m_gains, new_v_gains = adamw_step(
        gains, grad_gains, m_gains, v_gains, 0.0, gain_rate
    )
    return (
        output,
        grad_tokens,
        grad_attn,
        grad_gate_up,
        grad_down,
        grad_gains,
        new_attn,
        new_gate_up,
        new_down,
        new_gains,
        new_m_attn,
        new_v_attn,
        new_m_gate_up,
        new_v_gate_up,
        new_m_down,
        new_v_down,
        new_m_gains,
        new_v_gains,
    )


def solution(mesh):
    copies, places = mesh.devices.shape
    mesh = Mesh(mesh.devices.reshape(copies // 2, 2, 2, places // 2), DP + FSDP)
    matrix, vector = P(DP + FSDP, None), P(DP + FSDP)
    in_specs = (matrix, vector) + (matrix,) * 13
    return jax.shard_map(
        per_device, mesh=mesh, in_specs=in_specs, out_specs=(matrix,) * 18, check_vma=False
    )
```

```python
import functools
import math

import jax
import jax.numpy as jnp
from jax import lax
from jax.experimental import pallas as pl
from jax.experimental.pallas import tpu as pltpu
from jax.experimental.layout import Layout, with_layout_constraint
from jax.sharding import Mesh
from jax.sharding import PartitionSpec as P

HEAD_DIM = 128

norm_eps = 1e-06
rope_base = 500000.0
learn_rate = 0.004
gain_rate = 0.25
beta_one = 0.9
beta_two = 0.95
decay_rate = 0.1
adam_eps = 1e-08
correct_one = 1.0 - beta_one**2
correct_two = 1.0 - beta_two**2
neg_large = -1e30
bf16 = jnp.bfloat16
f32 = jnp.float32
TILE = 512
ALL_VMEM = 60 * 1024 * 1024


def mm(left, right, dims):
    return lax.dot_general(left, right, (dims, ((), ())), preferred_element_type=f32)


def adamw_step(weight, gradient, moment, second, decay_coef, rate_value):
    moment_new = beta_one * moment + (1.0 - beta_one) * gradient
    second_new = beta_two * second + (1.0 - beta_two) * gradient * gradient
    step_ratio = moment_new / correct_one / (jnp.sqrt(second_new / correct_two) + adam_eps)
    return (
        weight * (1.0 - rate_value * decay_coef) - rate_value * step_ratio,
        moment_new,
        second_new,
    )


def spread_body(tile, *refs):
    out = refs[-1]
    if tile:
        for i in range(refs[0].shape[1] // tile):
            for g, ref in enumerate(refs[:-1]):
                start = (i * len(refs[:-1]) + g) * tile
                out[:, start : start + tile] = ref[:, i * tile : (i + 1) * tile].astype(bf16)
        return
    start = 0
    for ref in refs[:-1]:
        out[:, start : start + ref.shape[1]] = ref[...].astype(bf16)
        start += ref.shape[1]


def spread_kernel(weight, groups, count, tile):
    owned, columns = weight.shape
    size = columns // (groups * count)
    specs = [
        pl.BlockSpec((owned, size), lambda f, g=g: (0, g * count + f)) for g in range(groups)
    ]
    operands = [weight] * groups
    wide = groups * size
    return pl.pallas_call(
        functools.partial(spread_body, tile),
        grid=(count,),
        in_specs=specs,
        out_specs=pl.BlockSpec((owned, wide), lambda f: (f, 0)),
        out_shape=jax.ShapeDtypeStruct((count * owned, wide), bf16),
        compiler_params=pltpu.CompilerParams(vmem_limit_bytes=40 * 1024 * 1024),
        cost_estimate=pl.CostEstimate(
            flops=0, bytes_accessed=6 * owned * columns, transcendentals=0
        ),
    )(*operands)


def adamw_body(tile, *refs):
    grad_in, weight, moment, second, grad_out, new_weight, new_moment, new_second = refs
    if tile:
        groups = grad_in.shape[1] // weight.shape[1]
        for i in range(weight.shape[1] // tile):
            start = pl.multiple_of((i * groups + pl.program_id(1)) * tile, tile)
            grad_out[:, i * tile : (i + 1) * tile] = grad_in[:, pl.ds(start, tile)].astype(f32)
    else:
        grad_out[...] = grad_in[...].astype(f32)
    new_weight[...], new_moment[...], new_second[...] = adamw_step(
        weight[...], grad_out[...], moment[...], second[...], decay_rate, learn_rate
    )


def adamw_kernel(gradient, weight, moment, second, groups, count, tile=0):
    owned, columns = weight.shape
    size = columns // (groups * count)
    whole = pl.BlockSpec((owned, size), lambda f, g: (0, g * count + f))
    if tile:
        grad_spec = pl.BlockSpec((owned, groups * size), lambda f, g: (f, 0))
    else:
        grad_spec = pl.BlockSpec((owned, size), lambda f, g: (f, g))
    return pl.pallas_call(
        functools.partial(adamw_body, tile),
        grid=(count, groups),
        in_specs=[grad_spec, whole, whole, whole],
        out_specs=[whole] * 4,
        out_shape=[jax.ShapeDtypeStruct(weight.shape, f32)] * 4,
        compiler_params=pltpu.CompilerParams(vmem_limit_bytes=40 * 1024 * 1024),
        cost_estimate=pl.CostEstimate(
            flops=12 * owned * columns, bytes_accessed=30 * owned * columns, transcendentals=0
        ),
    )(gradient, weight, moment, second)


def dot(left, right, left_dim, right_dim):
    return lax.dot_general(
        left, right, (((left_dim,), (right_dim,)), ((), ())), preferred_element_type=f32
    )


def visible(first_ref, low, high):
    shape = (high - low, high)
    row = lax.broadcasted_iota(jnp.int32, shape, 0) + low
    column = lax.broadcasted_iota(jnp.int32, shape, 1)
    return (column <= row) & (column >= first_ref[low:high, :])


def attend_body(block, scale, *refs):
    query_in, key_in, value_in, inverse, gain, cosine, sine, first = refs[:8]
    query_out, key_out, value_out, attended, lse = refs[8:]

    def turned(values, column):
        normed = values * inverse[:, column : column + 1] * gain[column : column + 1, :]
        return (normed * cosine[...] + pltpu.roll(normed, HEAD_DIM // 2, 1) * sine[...]).astype(bf16)

    query_out[...] = turned(query_in[...], 0)
    key_out[...] = turned(key_in[...], 1)
    value_out[...] = value_in[...].astype(bf16)
    for low in range(0, query_in.shape[0], block):
        high = low + block
        scores = dot(query_out[low:high, :], key_out[:high, :], 1, 1) * scale
        scores = jnp.where(visible(first, low, high), scores, neg_large)
        top = jnp.max(scores, axis=1, keepdims=True)
        weights = jnp.exp(scores - top)
        denom = jnp.sum(weights, axis=1, keepdims=True)
        attended[low:high, :] = (
            dot(weights.astype(bf16), value_out[:high, :], 1, 0) / denom
        ).astype(bf16)
        lse[0, low:high, :] = top + jnp.log(denom)


def attend_back_body(block, scale, *refs):
    query, key, value, attended, grad_att, lse = refs[:6]
    query_in, key_in, inverse, gain, cosine, sine, first = refs[6:13]
    query_grad, key_grad, value_grad, gain_grad, inner = refs[13:18]
    key_sum, value_sum = refs[18:]
    grad_low = grad_att
    delta = jnp.sum(
        grad_low[...].astype(f32) * attended[...].astype(f32), axis=1, keepdims=True
    )
    key_sum[...] = jnp.zeros_like(key_sum)
    value_sum[...] = jnp.zeros_like(value_sum)
    for low in range(0, query.shape[0], block):
        high = low + block
        scores = dot(query[low:high, :], key[:high, :], 1, 1) * scale
        prob = jnp.where(
            visible(first, low, high), jnp.exp(scores - lse[0, low:high, :]), 0.0
        )
        grad_prob = dot(grad_low[low:high, :], value[:high, :], 1, 1)
        grad_scores = (prob * (grad_prob - delta[low:high, :])).astype(bf16)
        query_grad[low:high, :] = dot(grad_scores, key[:high, :], 1, 0) * scale
        key_sum[:high, :] += dot(grad_scores, query[low:high, :], 0, 0)
        value_sum[:high, :] += dot(prob.astype(bf16), grad_low[low:high, :], 0, 0)
    value_grad[...] = value_sum[...].astype(bf16)
    lane = lax.broadcasted_iota(jnp.int32, inner.shape, 1)

    @pl.when(pl.program_id(0) == 0)
    def _():
        inner[...] = jnp.zeros_like(inner)

    gain_grad[...] = jnp.zeros_like(gain_grad)
    for column, turned, raw, out in (
        (0, query_grad[...], query_in, query_grad),
        (1, key_sum[...] * scale, key_in, key_grad),
    ):
        back = turned * cosine[...] - pltpu.roll(turned, HEAD_DIM // 2, 1) * sine[...]
        hat = raw[...] * inverse[:, column : column + 1]
        gain_grad[column : column + 1, :] = jnp.sum(back * hat, axis=0, keepdims=True)
        back = back * gain[column : column + 1, :]
        out[...] = back
        inner[...] += jnp.where(
            lane == column, jnp.sum(back * hat, axis=1, keepdims=True), 0.0
        )


def attend_kernels(length, heads):
    block = math.gcd(length, 256)
    scale = 1.0 / math.sqrt(HEAD_DIM)
    part = heads * HEAD_DIM

    def own(shift=0):
        return pl.BlockSpec((length, HEAD_DIM), lambda h: (0, h + shift))

    def same(width):
        return pl.BlockSpec((length, width), lambda h: (0, 0))

    gain_spec = pl.BlockSpec((8, HEAD_DIM), lambda h: (0, h))
    lse_spec = pl.BlockSpec((1, length, 1), lambda h: (h, 0, 0))
    tables = [same(2), gain_spec, same(HEAD_DIM), same(HEAD_DIM), same(1)]
    low_shape = jax.ShapeDtypeStruct((length, part), bf16)
    wide_shape = jax.ShapeDtypeStruct((length, part), f32)
    work = 2 * heads * length * length * HEAD_DIM
    params = pltpu.CompilerParams(vmem_limit_bytes=48 * 1024 * 1024)

    def forward(qkv, *rest):
        return pl.pallas_call(
            functools.partial(attend_body, block, scale),
            grid=(heads,),
            in_specs=[own(), own(heads), own(2 * heads)] + tables,
            out_specs=[own()] * 4 + [lse_spec],
            out_shape=[low_shape] * 4 + [jax.ShapeDtypeStruct((heads, length, 1), f32)],
            compiler_params=params,
            cost_estimate=pl.CostEstimate(
                flops=2 * work, bytes_accessed=20 * length * part, transcendentals=0
            ),
        )(qkv, qkv, qkv, *rest)

    def backward(query, key, value, attended, grad_att, lse, qkv, *rest):
        return pl.pallas_call(
            functools.partial(attend_back_body, block, scale),
            grid=(heads,),
            in_specs=[own()] * 5 + [lse_spec, own(), own(heads)] + tables,
            out_specs=[own()] * 3 + [gain_spec, same(HEAD_DIM)],
            out_shape=[
                wide_shape,
                wide_shape,
                low_shape,
                jax.ShapeDtypeStruct((8, part), f32),
                jax.ShapeDtypeStruct((length, HEAD_DIM), f32),
            ],
            scratch_shapes=[
                pltpu.VMEM((length, HEAD_DIM), f32),
                pltpu.VMEM((length, HEAD_DIM), f32),
            ],
            compiler_params=params,
            cost_estimate=pl.CostEstimate(
                flops=5 * work, bytes_accessed=30 * length * part, transcendentals=0
            ),
        )(query, key, value, attended, grad_att, lse, qkv, qkv, *rest)

    return forward, backward


def qkv_back_body(query_grad, key_grad, value_grad, raw, inverse, inner, out):
    part = query_grad.shape[1]
    for column, grad in ((0, query_grad), (1, key_grad)):
        scale = inverse[:, column : column + 1]
        hat = raw[:, column * part : (column + 1) * part] * scale
        out[:, column * part : (column + 1) * part] = (
            scale * (grad[...] - hat * inner[:, column : column + 1])
        ).astype(bf16)
    out[:, 2 * part :] = value_grad[...]


def qkv_back(query_grad, key_grad, value_grad, qkv, inverse, inner):
    length, part = query_grad.shape
    rows = math.gcd(length, 256)

    def spec(width):
        return pl.BlockSpec((rows, width), lambda i: (i, 0))

    return pl.pallas_call(
        qkv_back_body,
        grid=(length // rows,),
        in_specs=[spec(part)] * 3 + [spec(2 * part), spec(2), spec(2)],
        out_specs=spec(3 * part),
        out_shape=jax.ShapeDtypeStruct((length, 3 * part), bf16),
        compiler_params=pltpu.CompilerParams(vmem_limit_bytes=ALL_VMEM),
        cost_estimate=pl.CostEstimate(
            flops=8 * length * part, bytes_accessed=24 * length * part, transcendentals=0
        ),
    )(query_grad, key_grad, value_grad, qkv, inverse, inner)


def attn_grad_body(token, grad_qkv, attended, grad_branch, *rest):
    out = rest[-1]
    wide = grad_qkv.shape[1]
    for low, high, left, right in (
        (0, wide, token, grad_qkv),
        (wide, out.shape[1], attended, grad_branch),
    ):
        value = dot(left[...], right[...], 1, 0)
        if len(rest) > 1:
            value = value + rest[0][:, low:high].astype(f32)
        out[:, low:high] = value.astype(bf16)


def attn_grad(token, grad_qkv, attended, grad_branch, *other):
    width, length = token.shape
    rows = math.gcd(width, 512)
    columns = grad_qkv.shape[1] + grad_branch.shape[1]

    def row_spec(wide):
        return pl.BlockSpec((rows, wide), lambda i: (i, 0))

    def whole(array):
        return pl.BlockSpec(array.shape, lambda i: (0, 0))

    return pl.pallas_call(
        attn_grad_body,
        grid=(width // rows,),
        in_specs=[row_spec(length), whole(grad_qkv), row_spec(length), whole(grad_branch)]
        + [row_spec(columns)] * len(other),
        out_specs=row_spec(columns),
        out_shape=jax.ShapeDtypeStruct((width, columns), bf16),
        compiler_params=pltpu.CompilerParams(vmem_limit_bytes=ALL_VMEM),
        cost_estimate=pl.CostEstimate(
            flops=2 * width * length * columns,
            bytes_accessed=6 * width * length,
            transcendentals=0,
        ),
    )(token, grad_qkv, attended, grad_branch, *other)


def token_grad_body(place, grad_qkv, weight, grad_hidden, out):
    own = (pl.program_id(0) == place[0]).astype(f32)
    out[...] = (dot(grad_qkv[...], weight[...], 1, 1) + own * grad_hidden[...]).astype(bf16)


def token_grad(place, grad_qkv, weight, grad_hidden):
    length, wide = grad_qkv.shape
    width, part = weight.shape[0], grad_hidden.shape[1]
    return pl.pallas_call(
        token_grad_body,
        grid_spec=pltpu.PrefetchScalarGridSpec(
            num_scalar_prefetch=1,
            grid=(width // part,),
            in_specs=[
                pl.BlockSpec((length, wide), lambda j, place: (0, 0)),
                pl.BlockSpec((part, wide), lambda j, place: (j, 0)),
                pl.BlockSpec((length, part), lambda j, place: (0, 0)),
            ],
            out_specs=pl.BlockSpec((length, part), lambda j, place: (0, j)),
        ),
        out_shape=jax.ShapeDtypeStruct((length, width), bf16),
        compiler_params=pltpu.CompilerParams(vmem_limit_bytes=ALL_VMEM),
        cost_estimate=pl.CostEstimate(
            flops=2 * width * length * wide, bytes_accessed=8 * width * length, transcendentals=0
        ),
    )(place, grad_qkv, weight, grad_hidden)


def half_grad_body(left, right, *rest):
    value = dot(left[...], right[...], 1, 0)
    if len(rest) > 1:
        value = value + rest[0][...].astype(f32)
    rest[-1][...] = value.astype(bf16)


def half_grad(left, right, *other):
    rows, length = left.shape
    columns = right.shape[1]
    size = math.gcd(columns, 512)
    spec = pl.BlockSpec((rows, size), lambda j: (0, j))
    return pl.pallas_call(
        half_grad_body,
        grid=(columns // size,),
        in_specs=[
            pl.BlockSpec((rows, length), lambda j: (0, 0)),
            pl.BlockSpec((length, size), lambda j: (0, j)),
        ]
        + [spec] * len(other),
        out_specs=spec,
        out_shape=jax.ShapeDtypeStruct((rows, columns), bf16),
        compiler_params=pltpu.CompilerParams(vmem_limit_bytes=48 * 1024 * 1024),
        cost_estimate=pl.CostEstimate(
            flops=2 * rows * length * columns, bytes_accessed=4 * rows * columns, transcendentals=0
        ),
    )(left, right, *other)


def gate_up_body(hidden, weight, both, activ):
    value = dot(hidden[...], weight[...], 1, 0)
    gate, up = value[:, :TILE], value[:, TILE:]
    sigmoid = jax.nn.sigmoid(gate)
    silu = gate * sigmoid
    activ[...] = (silu * up).astype(bf16)
    both[:, :TILE] = up * sigmoid * (1.0 + gate * (1.0 - sigmoid))
    both[:, TILE:] = silu


def gate_up_back_body(grad_mlp, weight, both, out):
    grad = dot(grad_mlp[...], weight[...], 1, 0)
    for start in (0, TILE):
        out[:, start : start + TILE] = (grad * both[:, start : start + TILE]).astype(bf16)


def gate_up_kernels(length, width, wide):
    params = pltpu.CompilerParams(vmem_limit_bytes=48 * 1024 * 1024)
    rows_spec = pl.BlockSpec((length, width), lambda j: (0, 0))

    def columns(rows, size):
        return pl.BlockSpec((rows, size), lambda j: (0, j))

    def forward(hidden, weight):
        return pl.pallas_call(
            gate_up_body,
            grid=(wide // TILE,),
            in_specs=[rows_spec, columns(width, 2 * TILE)],
            out_specs=[columns(length, 2 * TILE), columns(length, TILE)],
            out_shape=[
                jax.ShapeDtypeStruct((length, 2 * wide), f32),
                jax.ShapeDtypeStruct((length, wide), bf16),
            ],
            compiler_params=params,
            cost_estimate=pl.CostEstimate(
                flops=4 * length * width * wide,
                bytes_accessed=10 * length * wide + 4 * width * wide,
                transcendentals=0,
            ),
        )(hidden, weight)

    def backward(grad_mlp, weight, both):
        return pl.pallas_call(
            gate_up_back_body,
            grid=(wide // TILE,),
            in_specs=[rows_spec, columns(width, TILE), columns(length, 2 * TILE)],
            out_specs=columns(length, 2 * TILE),
            out_shape=jax.ShapeDtypeStruct((length, 2 * wide), bf16),
            compiler_params=pltpu.CompilerParams(vmem_limit_bytes=ALL_VMEM),
            cost_estimate=pl.CostEstimate(
                flops=2 * length * width * wide,
                bytes_accessed=12 * length * wide + 2 * width * wide,
                transcendentals=0,
            ),
        )(grad_mlp, weight, both)

    return forward, backward


FSDP, DP = ("y", "x"), ("z", "core")


def order_body(values, other, out):
    pass


def order(values, other):
    anywhere = pl.BlockSpec(memory_space=pl.ANY)
    return pl.pallas_call(
        order_body,
        in_specs=[anywhere, anywhere],
        out_specs=anywhere,
        out_shape=jax.ShapeDtypeStruct(values.shape, values.dtype),
        input_output_aliases={0: 0},
    )(values, other)


def zero_after(other):
    first = other[(slice(0, 1),) * other.ndim].astype(f32).reshape(())
    return jnp.minimum(jnp.abs(first), 0.0).astype(jnp.int32)


class Copies:
    def __init__(self):
        self.count = lax.axis_size("z")

    def swap(self, values):
        return lax.ppermute(values, "core", [(0, 1), (1, 0)])

    def along(self, values):
        return [values] + [
            lax.ppermute(values, "z", [(i, (i + step) % self.count) for i in range(self.count)])
            for step in range(1, self.count)
        ]

    def gather(self, values):
        core, place = lax.axis_index("core"), lax.axis_index("z")
        other = self.swap(values)
        both = jnp.concatenate(
            [lax.select_n(core, values, other), lax.select_n(core, other, values)]
        )
        parts = self.along(both)
        return jnp.concatenate(
            [lax.select_n((place - z) % self.count, *parts) for z in range(self.count)]
        )

    def total(self, values):
        return sum(self.along(values + self.swap(values)))


class Plane:
    def __init__(self, count):
        self.count = count
        self.square = count == 4
        self.place = lax.axis_index(FSDP)

    def swap(self, values, bit):
        return lax.ppermute(values, FSDP, [(i, i ^ bit) for i in range(self.count)])

    def gather(self, block, axis, fill=0):
        if not self.square:
            return lax.all_gather(block, FSDP, axis=axis, tiled=True)
        other = 1 - axis
        size, cut = block.shape[axis], block.shape[other] // 2
        by_x, by_y = self.swap(block, 1), self.swap(block, 2)
        low = self.swap(lax.slice_in_dim(by_x, 0, cut, axis=other), 2)
        high = self.swap(lax.slice_in_dim(by_y, cut, 2 * cut, axis=other), 1)
        shape = list(block.shape)
        shape[axis] = size * 4
        out = jnp.full(shape, fill, block.dtype)
        for part, bit, offset in ((block, 0, 0), (by_x, 1, 0), (by_y, 2, 0), (low, 3, 0), (high, 3, cut)):
            start = [0, 0]
            start[axis] = (self.place ^ bit) * size
            start[other] = offset
            out = lax.dynamic_update_slice(out, part, start)
        return out

    def scatter(self, partial, axis, kind=f32, hop=0, last=(0, 0)):
        if not self.square:
            total = lax.psum_scatter(partial, FSDP, scatter_dimension=axis, tiled=True)
            return total.astype(f32)
        other = 1 - axis
        size, cut = partial.shape[axis] // 4, partial.shape[other] // 2
        place = self.place

        def piece(bit, offset, zero=0):
            start = [0, 0]
            start[axis] = (place ^ bit) * size + zero
            start[other] = offset
            extent = [0, 0]
            extent[axis] = size
            extent[other] = cut
            return lax.dynamic_slice(partial, start, extent)

        halves = []
        for (offset, first, second), zero in zip(((0, 1, 2), (cut, 2, 1)), last):
            relay = self.swap(piece(3, offset), first)
            mine = self.swap(piece(first, offset), first)
            relay = (piece(second, offset, hop).astype(f32) + relay.astype(f32)).astype(bf16)
            halves.append(
                piece(0, offset, zero).astype(f32) + mine.astype(f32) + self.swap(relay, second).astype(f32)
            )
        return jnp.concatenate([half.astype(kind) for half in halves], axis=other)

    def total(self, values):
        if not self.square:
            return lax.psum(values, FSDP)
        return values + self.swap(values, 1) + self.swap(values, 2) + self.swap(values, 3)

    def gather_small(self, values):
        if not self.square:
            return lax.all_gather(values, FSDP, axis=0, tiled=True)
        parts = [values] + [self.swap(values, bit) for bit in (1, 2, 3)]
        return jnp.concatenate(
            [
                lax.select_n(self.place ^ j, *parts)
                for j in range(4)
            ],
            axis=0,
        )


def per_device(
    tokens,
    positions,
    cotangent,
    w_attn,
    w_gate_up,
    w_down,
    gains,
    m_attn,
    v_attn,
    m_gate_up,
    v_gate_up,
    m_down,
    v_down,
    m_gains,
    v_gains,
):
    rows, width = tokens.shape
    owned = w_attn.shape[0]
    hidden = w_down.shape[1]
    count = lax.axis_size(FSDP)
    plane = Plane(count)
    place = plane.place
    length = rows * count
    part = width // count
    heads = part // HEAD_DIM
    wide = hidden // count
    scale = 1.0 / math.sqrt(HEAD_DIM)

    def spread(weight, groups, tile=0):
        block = spread_kernel(weight, groups, count, tile)
        return lax.all_to_all(block, FSDP, 0, 0, tiled=True)

    attn_all = lax.all_gather(spread(w_attn, 4), DP, axis=0, tiled=True)
    gate_up_all = lax.all_gather(spread(w_gate_up, 2, tile=TILE), DP, axis=0, tiled=True)
    down_all = lax.all_gather(spread(w_down, 1), DP, axis=0, tiled=True)
    qkv_weight = attn_all[:, : 3 * part]
    out_weight = attn_all[:, 3 * part : 4 * part]
    copies = Copies()
    gain_low = lax.reduce_precision(gains, exponent_bits=8, mantissa_bits=7)
    gain_values = copies.gather(plane.gather_small(jnp.transpose(gain_low).reshape(-1)))
    gain_values = jnp.transpose(gain_values.reshape(-1, 4, owned), (0, 2, 1)).reshape(width, 4)
    gain_part = lax.dynamic_slice_in_dim(gain_values, place * part, part, 0)

    token_full = plane.gather(tokens, 0)
    position_full = plane.gather_small(positions)
    cot_part = lax.all_to_all(
        cotangent.reshape(rows, count, part).transpose(1, 0, 2).reshape(count * rows, part),
        FSDP,
        0,
        0,
        tiled=True,
    ).astype(f32)

    half_dim = HEAD_DIM // 2
    frequency = jnp.exp(
        jnp.arange(half_dim, dtype=f32) * (-2.0 * math.log(rope_base) / HEAD_DIM)
    )
    angles = position_full.astype(f32)[:, None] * frequency[None, :]
    cosine, sine = jnp.cos(angles), jnp.sin(angles)
    cosine = jnp.concatenate([cosine, cosine], axis=1)
    sine = jnp.concatenate([-sine, sine], axis=1)
    first_key = (jnp.arange(length, dtype=jnp.int32) - position_full)[:, None]
    gain_rows = jnp.pad(jnp.transpose(gain_part), ((0, 4), (0, 0)))
    attend, attend_back = attend_kernels(length, heads)

    qkv = mm(token_full, qkv_weight, ((1,), (0,)))
    query_raw, key_raw = qkv[:, :part], qkv[:, part : 2 * part]
    squares = plane.total(
        jnp.concatenate([jnp.sum(query_raw * query_raw, axis=1), jnp.sum(key_raw * key_raw, axis=1)])
    )
    inverse = jnp.transpose(lax.rsqrt(squares / width + norm_eps).reshape(2, length))
    tables = (inverse, gain_rows, cosine, sine, first_key)
    query, key, value, attended_low, lse = attend(qkv, *tables)
    attended_full = plane.gather(attended_low, 1, 1)

    branch = mm(attended_full, out_weight, ((1,), (0,)))
    branch_inv = lax.rsqrt(plane.total(jnp.sum(branch * branch, axis=1)) / width + norm_eps)[:, None]
    branch_hat = branch * branch_inv
    token_part = lax.dynamic_slice_in_dim(token_full, place * part, part, 1).astype(f32)
    hidden_low = (token_part + branch_hat * gain_part[None, :, 2]).astype(bf16)
    hidden_full = plane.gather(hidden_low, 1, 2)

    core = lax.axis_index("core")
    share = width // (2 * copies.count)

    def sides(array):
        return [
            jnp.transpose(
                jnp.concatenate(
                    [
                        lax.dynamic_slice_in_dim(array, (2 * z + index) * share, share, 1)
                        for z in range(copies.count)
                    ],
                    axis=1,
                )
            )
            for index in (1 - core, core)
        ]

    other_side, own_side = sides(hidden_full)
    token_sides, attended_sides = sides(token_full), sides(attended_full)
    for early in (other_side, own_side, *token_sides, *attended_sides, cot_part):
        hidden_full = order(hidden_full, early)
    gate_up, gate_up_back = gate_up_kernels(length, width, wide)
    both, activ = gate_up(hidden_full, gate_up_all)
    mlp = plane.scatter(mm(activ, down_all, ((1,), (1,))).astype(bf16), 0)
    mlp_inv = lax.rsqrt(jnp.mean(mlp * mlp, axis=1, keepdims=True) + norm_eps)
    mlp_hat = mlp * mlp_inv
    hidden_rows = lax.dynamic_slice_in_dim(hidden_full, place * rows, rows, 0).astype(f32)
    output = (hidden_rows + mlp_hat * gain_values[None, :, 3]).astype(bf16)

    grad_out = cotangent.astype(f32)
    scaled = grad_out * gain_values[None, :, 3]
    grad_mlp = mlp_inv * (scaled - mlp_hat * jnp.mean(scaled * mlp_hat, axis=1, keepdims=True))
    grad_gain_mlp = jnp.sum(grad_out * mlp_hat, axis=0)
    by_rows = Layout(major_to_minor=(0, 1))
    grad_mlp_full = with_layout_constraint(
        plane.gather(with_layout_constraint(grad_mlp.astype(bf16), by_rows), 0, 3), by_rows
    )

    def exchanged(mine, *wait):
        for other in wait:
            mine = order(mine, other)
        return lax.all_to_all(mine, FSDP, 0, 0, tiled=True)

    down_partial = mm(grad_mlp_full, activ, ((0,), (0,))).astype(bf16)
    down_mine = lax.psum_scatter(down_partial, DP, scatter_dimension=0, tiled=True)
    grad_gate_up_low = gate_up_back(grad_mlp_full, down_all, both)

    send = half_grad(other_side, grad_gate_up_low)
    got = copies.swap(send)
    late = order(grad_gate_up_low, send)
    hidden_partial = mm(late, gate_up_all, ((1,), (1,))).astype(bf16)
    grad_hidden = cot_part + plane.scatter(hidden_partial, 1)
    gate_up_partial = half_grad(order(own_side, hidden_partial[:16, :128]), late, got)
    gate_up_mine = lax.psum_scatter(gate_up_partial, "z", scatter_dimension=0, tiled=True)

    scaled = grad_hidden * gain_part[None, :, 2]
    grad_gain_attn = jnp.sum(grad_hidden * branch_hat, axis=0)
    inner = plane.total(jnp.sum(scaled * branch_hat, axis=1))[:, None] / width
    grad_branch = (branch_inv * (scaled - branch_hat * inner)).astype(bf16)
    grad_branch = order(grad_branch, down_mine)
    grad_att = plane.scatter(
        mm(grad_branch, out_weight, ((1,), (1,))).astype(bf16), 1, bf16
    )
    query_grad, key_grad, value_grad, gain_grad, inner = attend_back(
        query, key, value, attended_low, grad_att, lse, qkv, *tables
    )
    inner = plane.total(jnp.concatenate([inner[:, 0], inner[:, 1]])) / width
    inner = jnp.transpose(inner.reshape(2, length))
    grad_qkv_low = qkv_back(query_grad, key_grad, value_grad, qkv, inverse, inner)

    own_gains = jnp.stack([gain_grad[0], gain_grad[1], grad_gain_attn])
    gain_sums = jnp.concatenate([jnp.zeros((3, width), f32), grad_gain_mlp[None]])
    gain_sums = lax.dynamic_update_slice(gain_sums, own_gains, (0, place * part)).reshape(-1)
    gain_sums = plane.total(copies.total(gain_sums)).reshape(4, width)
    owner = lax.axis_index(DP + FSDP)
    grad_gains = jnp.transpose(lax.dynamic_slice_in_dim(gain_sums, owner * owned, owned, 1))
    send = attn_grad(token_sides[0], grad_qkv_low, attended_sides[0], grad_branch)
    got = copies.swap(send)
    late = order(grad_qkv_low, send)
    back = token_grad(jnp.full((1,), place), late, attn_all, grad_hidden)
    late = order(late, back)
    attn_partial = attn_grad(token_sides[1], late, attended_sides[1], grad_branch, got)
    down_part = exchanged(down_mine, grad_qkv_low)
    attn_partial = order(order(attn_partial, down_part), gate_up_mine)
    attn_mine = lax.psum_scatter(attn_partial, "z", scatter_dimension=0, tiled=True)
    gate_up_part = exchanged(gate_up_mine, attn_partial)
    grad_down, new_down, new_m_down, new_v_down = adamw_kernel(
        order(down_part, attn_partial), w_down, m_down, v_down, 1, count
    )
    grad_tokens = plane.scatter(
        back,
        0,
        hop=zero_after(new_down),
        last=(zero_after(gate_up_part), zero_after(grad_gains)),
    )
    attn_mine = order(order(attn_mine, grad_tokens), new_down)
    attn_part = exchanged(attn_mine)
    grad_gate_up, new_gate_up, new_m_gate_up, new_v_gate_up = adamw_kernel(
        order(gate_up_part, attn_mine), w_gate_up, m_gate_up, v_gate_up, 2, count, TILE
    )
    grad_attn, new_attn, new_m_attn, new_v_attn = adamw_kernel(
        order(attn_part, new_gate_up), w_attn, m_attn, v_attn, 4, count
    )
    new_gains, new_m_gains, new_v_gains = adamw_step(
        gains, grad_gains, m_gains, v_gains, 0.0, gain_rate
    )
    return (
        output,
        grad_tokens,
        grad_attn,
        grad_gate_up,
        grad_down,
        grad_gains,
        new_attn,
        new_gate_up,
        new_down,
        new_gains,
        new_m_attn,
        new_v_attn,
        new_m_gate_up,
        new_v_gate_up,
        new_m_down,
        new_v_down,
        new_m_gains,
        new_v_gains,
    )


def solution(mesh):
    copies, places = mesh.devices.shape
    mesh = Mesh(mesh.devices.reshape(copies // 2, 2, 2, places // 2), DP + FSDP)
    matrix, vector = P(DP + FSDP, None), P(DP + FSDP)
    in_specs = (matrix, vector) + (matrix,) * 13
    return jax.shard_map(
        per_device, mesh=mesh, in_specs=in_specs, out_specs=(matrix,) * 18, check_vma=False
    )
```

```python
import functools
import math

import jax
import jax.numpy as jnp
from jax import lax
from jax.experimental import pallas as pl
from jax.experimental.pallas import tpu as pltpu
from jax.experimental.layout import Layout, with_layout_constraint
from jax.sharding import Mesh
from jax.sharding import PartitionSpec as P

HEAD_DIM = 128

norm_eps = 1e-06
rope_base = 500000.0
learn_rate = 0.004
gain_rate = 0.25
beta_one = 0.9
beta_two = 0.95
decay_rate = 0.1
adam_eps = 1e-08
correct_one = 1.0 - beta_one**2
correct_two = 1.0 - beta_two**2
neg_large = -1e30
bf16 = jnp.bfloat16
f32 = jnp.float32
TILE = 512
ALL_VMEM = 60 * 1024 * 1024


def mm(left, right, dims):
    return lax.dot_general(left, right, (dims, ((), ())), preferred_element_type=f32)


def adamw_step(weight, gradient, moment, second, decay_coef, rate_value):
    moment_new = beta_one * moment + (1.0 - beta_one) * gradient
    second_new = beta_two * second + (1.0 - beta_two) * gradient * gradient
    step_ratio = moment_new / correct_one / (jnp.sqrt(second_new / correct_two) + adam_eps)
    return (
        weight * (1.0 - rate_value * decay_coef) - rate_value * step_ratio,
        moment_new,
        second_new,
    )


def spread_body(tile, *refs):
    out = refs[-1]
    if tile:
        for i in range(refs[0].shape[1] // tile):
            for g, ref in enumerate(refs[:-1]):
                start = (i * len(refs[:-1]) + g) * tile
                out[:, start : start + tile] = ref[:, i * tile : (i + 1) * tile].astype(bf16)
        return
    start = 0
    for ref in refs[:-1]:
        out[:, start : start + ref.shape[1]] = ref[...].astype(bf16)
        start += ref.shape[1]


def spread_kernel(weight, groups, count, tile):
    owned, columns = weight.shape
    size = columns // (groups * count)
    specs = [
        pl.BlockSpec((owned, size), lambda f, g=g: (0, g * count + f)) for g in range(groups)
    ]
    operands = [weight] * groups
    wide = groups * size
    return pl.pallas_call(
        functools.partial(spread_body, tile),
        grid=(count,),
        in_specs=specs,
        out_specs=pl.BlockSpec((owned, wide), lambda f: (f, 0)),
        out_shape=jax.ShapeDtypeStruct((count * owned, wide), bf16),
        compiler_params=pltpu.CompilerParams(vmem_limit_bytes=40 * 1024 * 1024),
        cost_estimate=pl.CostEstimate(
            flops=0, bytes_accessed=6 * owned * columns, transcendentals=0
        ),
    )(*operands)


def adamw_body(tile, *refs):
    grad_in, weight, moment, second, grad_out, new_weight, new_moment, new_second = refs
    if tile:
        groups = grad_in.shape[1] // weight.shape[1]
        for i in range(weight.shape[1] // tile):
            start = pl.multiple_of((i * groups + pl.program_id(1)) * tile, tile)
            grad_out[:, i * tile : (i + 1) * tile] = grad_in[:, pl.ds(start, tile)].astype(f32)
    else:
        grad_out[...] = grad_in[...].astype(f32)
    new_weight[...], new_moment[...], new_second[...] = adamw_step(
        weight[...], grad_out[...], moment[...], second[...], decay_rate, learn_rate
    )


def adamw_kernel(gradient, weight, moment, second, groups, count, tile=0):
    owned, columns = weight.shape
    size = columns // (groups * count)
    whole = pl.BlockSpec((owned, size), lambda f, g: (0, g * count + f))
    if tile:
        grad_spec = pl.BlockSpec((owned, groups * size), lambda f, g: (f, 0))
    else:
        grad_spec = pl.BlockSpec((owned, size), lambda f, g: (f, g))
    return pl.pallas_call(
        functools.partial(adamw_body, tile),
        grid=(count, groups),
        in_specs=[grad_spec, whole, whole, whole],
        out_specs=[whole] * 4,
        out_shape=[jax.ShapeDtypeStruct(weight.shape, f32)] * 4,
        compiler_params=pltpu.CompilerParams(vmem_limit_bytes=40 * 1024 * 1024),
        cost_estimate=pl.CostEstimate(
            flops=12 * owned * columns, bytes_accessed=30 * owned * columns, transcendentals=0
        ),
    )(gradient, weight, moment, second)


def dot(left, right, left_dim, right_dim):
    return lax.dot_general(
        left, right, (((left_dim,), (right_dim,)), ((), ())), preferred_element_type=f32
    )


def visible(first_ref, low, high):
    shape = (high - low, high)
    row = lax.broadcasted_iota(jnp.int32, shape, 0) + low
    column = lax.broadcasted_iota(jnp.int32, shape, 1)
    return (column <= row) & (column >= first_ref[low:high, :])


def attend_body(block, scale, *refs):
    query_in, key_in, value_in, inverse, gain, cosine, sine, first = refs[:8]
    query_out, key_out, value_out, attended, lse = refs[8:]

    def turned(values, column):
        normed = values * inverse[:, column : column + 1] * gain[column : column + 1, :]
        return (normed * cosine[...] + pltpu.roll(normed, HEAD_DIM // 2, 1) * sine[...]).astype(bf16)

    query_out[...] = turned(query_in[...], 0)
    key_out[...] = turned(key_in[...], 1)
    value_out[...] = value_in[...].astype(bf16)
    for low in range(0, query_in.shape[0], block):
        high = low + block
        scores = dot(query_out[low:high, :], key_out[:high, :], 1, 1) * scale
        scores = jnp.where(visible(first, low, high), scores, neg_large)
        top = jnp.max(scores, axis=1, keepdims=True)
        weights = jnp.exp(scores - top)
        denom = jnp.sum(weights, axis=1, keepdims=True)
        attended[low:high, :] = (
            dot(weights.astype(bf16), value_out[:high, :], 1, 0) / denom
        ).astype(bf16)
        lse[0, low:high, :] = top + jnp.log(denom)


def attend_back_body(block, scale, *refs):
    query, key, value, attended, grad_att, lse = refs[:6]
    query_in, key_in, inverse, gain, cosine, sine, first = refs[6:13]
    query_grad, key_grad, value_grad, gain_grad, inner = refs[13:18]
    key_sum, value_sum = refs[18:]
    grad_low = grad_att
    delta = jnp.sum(
        grad_low[...].astype(f32) * attended[...].astype(f32), axis=1, keepdims=True
    )
    key_sum[...] = jnp.zeros_like(key_sum)
    value_sum[...] = jnp.zeros_like(value_sum)
    for low in range(0, query.shape[0], block):
        high = low + block
        scores = dot(query[low:high, :], key[:high, :], 1, 1) * scale
        prob = jnp.where(
            visible(first, low, high), jnp.exp(scores - lse[0, low:high, :]), 0.0
        )
        grad_prob = dot(grad_low[low:high, :], value[:high, :], 1, 1)
        grad_scores = (prob * (grad_prob - delta[low:high, :])).astype(bf16)
        query_grad[low:high, :] = dot(grad_scores, key[:high, :], 1, 0) * scale
        key_sum[:high, :] += dot(grad_scores, query[low:high, :], 0, 0)
        value_sum[:high, :] += dot(prob.astype(bf16), grad_low[low:high, :], 0, 0)
    value_grad[...] = value_sum[...].astype(bf16)
    lane = lax.broadcasted_iota(jnp.int32, inner.shape, 1)

    @pl.when(pl.program_id(0) == 0)
    def _():
        inner[...] = jnp.zeros_like(inner)

    gain_grad[...] = jnp.zeros_like(gain_grad)
    for column, turned, raw, out in (
        (0, query_grad[...], query_in, query_grad),
        (1, key_sum[...] * scale, key_in, key_grad),
    ):
        back = turned * cosine[...] - pltpu.roll(turned, HEAD_DIM // 2, 1) * sine[...]
        hat = raw[...] * inverse[:, column : column + 1]
        gain_grad[column : column + 1, :] = jnp.sum(back * hat, axis=0, keepdims=True)
        back = back * gain[column : column + 1, :]
        out[...] = back
        inner[...] += jnp.where(
            lane == column, jnp.sum(back * hat, axis=1, keepdims=True), 0.0
        )


def attend_kernels(length, heads):
    block = math.gcd(length, 256)
    scale = 1.0 / math.sqrt(HEAD_DIM)
    part = heads * HEAD_DIM

    def own(shift=0):
        return pl.BlockSpec((length, HEAD_DIM), lambda h: (0, h + shift))

    def same(width):
        return pl.BlockSpec((length, width), lambda h: (0, 0))

    gain_spec = pl.BlockSpec((8, HEAD_DIM), lambda h: (0, h))
    lse_spec = pl.BlockSpec((1, length, 1), lambda h: (h, 0, 0))
    tables = [same(2), gain_spec, same(HEAD_DIM), same(HEAD_DIM), same(1)]
    low_shape = jax.ShapeDtypeStruct((length, part), bf16)
    wide_shape = jax.ShapeDtypeStruct((length, part), f32)
    work = 2 * heads * length * length * HEAD_DIM
    params = pltpu.CompilerParams(vmem_limit_bytes=48 * 1024 * 1024)

    def forward(qkv, *rest):
        return pl.pallas_call(
            functools.partial(attend_body, block, scale),
            grid=(heads,),
            in_specs=[own(), own(heads), own(2 * heads)] + tables,
            out_specs=[own()] * 4 + [lse_spec],
            out_shape=[low_shape] * 4 + [jax.ShapeDtypeStruct((heads, length, 1), f32)],
            compiler_params=params,
            cost_estimate=pl.CostEstimate(
                flops=2 * work, bytes_accessed=20 * length * part, transcendentals=0
            ),
        )(qkv, qkv, qkv, *rest)

    def backward(query, key, value, attended, grad_att, lse, qkv, *rest):
        return pl.pallas_call(
            functools.partial(attend_back_body, block, scale),
            grid=(heads,),
            in_specs=[own()] * 5 + [lse_spec, own(), own(heads)] + tables,
            out_specs=[own()] * 3 + [gain_spec, same(HEAD_DIM)],
            out_shape=[
                wide_shape,
                wide_shape,
                low_shape,
                jax.ShapeDtypeStruct((8, part), f32),
                jax.ShapeDtypeStruct((length, HEAD_DIM), f32),
            ],
            scratch_shapes=[
                pltpu.VMEM((length, HEAD_DIM), f32),
                pltpu.VMEM((length, HEAD_DIM), f32),
            ],
            compiler_params=params,
            cost_estimate=pl.CostEstimate(
                flops=5 * work, bytes_accessed=30 * length * part, transcendentals=0
            ),
        )(query, key, value, attended, grad_att, lse, qkv, qkv, *rest)

    return forward, backward


def qkv_back_body(query_grad, key_grad, value_grad, raw, inverse, inner, out):
    part = query_grad.shape[1]
    for column, grad in ((0, query_grad), (1, key_grad)):
        scale = inverse[:, column : column + 1]
        hat = raw[:, column * part : (column + 1) * part] * scale
        out[:, column * part : (column + 1) * part] = (
            scale * (grad[...] - hat * inner[:, column : column + 1])
        ).astype(bf16)
    out[:, 2 * part :] = value_grad[...]


def qkv_back(query_grad, key_grad, value_grad, qkv, inverse, inner):
    length, part = query_grad.shape
    rows = math.gcd(length, 256)

    def spec(width):
        return pl.BlockSpec((rows, width), lambda i: (i, 0))

    return pl.pallas_call(
        qkv_back_body,
        grid=(length // rows,),
        in_specs=[spec(part)] * 3 + [spec(2 * part), spec(2), spec(2)],
        out_specs=spec(3 * part),
        out_shape=jax.ShapeDtypeStruct((length, 3 * part), bf16),
        compiler_params=pltpu.CompilerParams(vmem_limit_bytes=ALL_VMEM),
        cost_estimate=pl.CostEstimate(
            flops=8 * length * part, bytes_accessed=24 * length * part, transcendentals=0
        ),
    )(query_grad, key_grad, value_grad, qkv, inverse, inner)


def attn_grad_body(token, grad_qkv, attended, grad_branch, *rest):
    out = rest[-1]
    wide = grad_qkv.shape[1]
    for low, high, left, right in (
        (0, wide, token, grad_qkv),
        (wide, out.shape[1], attended, grad_branch),
    ):
        value = dot(left[...], right[...], 1, 0)
        if len(rest) > 1:
            value = value + rest[0][:, low:high].astype(f32)
        out[:, low:high] = value.astype(bf16)


def attn_grad(token, grad_qkv, attended, grad_branch, *other):
    width, length = token.shape
    rows = math.gcd(width, 512)
    columns = grad_qkv.shape[1] + grad_branch.shape[1]

    def row_spec(wide):
        return pl.BlockSpec((rows, wide), lambda i: (i, 0))

    def whole(array):
        return pl.BlockSpec(array.shape, lambda i: (0, 0))

    return pl.pallas_call(
        attn_grad_body,
        grid=(width // rows,),
        in_specs=[row_spec(length), whole(grad_qkv), row_spec(length), whole(grad_branch)]
        + [row_spec(columns)] * len(other),
        out_specs=row_spec(columns),
        out_shape=jax.ShapeDtypeStruct((width, columns), bf16),
        compiler_params=pltpu.CompilerParams(vmem_limit_bytes=ALL_VMEM),
        cost_estimate=pl.CostEstimate(
            flops=2 * width * length * columns,
            bytes_accessed=6 * width * length,
            transcendentals=0,
        ),
    )(token, grad_qkv, attended, grad_branch, *other)


def token_grad_body(place, grad_qkv, weight, grad_hidden, out):
    own = (pl.program_id(0) == place[0]).astype(f32)
    out[...] = (dot(grad_qkv[...], weight[...], 1, 1) + own * grad_hidden[...]).astype(bf16)


def token_grad(place, grad_qkv, weight, grad_hidden):
    length, wide = grad_qkv.shape
    width, part = weight.shape[0], grad_hidden.shape[1]
    return pl.pallas_call(
        token_grad_body,
        grid_spec=pltpu.PrefetchScalarGridSpec(
            num_scalar_prefetch=1,
            grid=(width // part,),
            in_specs=[
                pl.BlockSpec((length, wide), lambda j, place: (0, 0)),
                pl.BlockSpec((part, wide), lambda j, place: (j, 0)),
                pl.BlockSpec((length, part), lambda j, place: (0, 0)),
            ],
            out_specs=pl.BlockSpec((length, part), lambda j, place: (0, j)),
        ),
        out_shape=jax.ShapeDtypeStruct((length, width), bf16),
        compiler_params=pltpu.CompilerParams(vmem_limit_bytes=ALL_VMEM),
        cost_estimate=pl.CostEstimate(
            flops=2 * width * length * wide, bytes_accessed=8 * width * length, transcendentals=0
        ),
    )(place, grad_qkv, weight, grad_hidden)


def half_grad_body(left, right, *rest):
    value = dot(left[...], right[...], 1, 0)
    if len(rest) > 1:
        value = value + rest[0][...].astype(f32)
    rest[-1][...] = value.astype(bf16)


def half_grad(left, right, *other):
    rows, length = left.shape
    columns = right.shape[1]
    size = math.gcd(columns, 512)
    spec = pl.BlockSpec((rows, size), lambda j: (0, j))
    return pl.pallas_call(
        half_grad_body,
        grid=(columns // size,),
        in_specs=[
            pl.BlockSpec((rows, length), lambda j: (0, 0)),
            pl.BlockSpec((length, size), lambda j: (0, j)),
        ]
        + [spec] * len(other),
        out_specs=spec,
        out_shape=jax.ShapeDtypeStruct((rows, columns), bf16),
        compiler_params=pltpu.CompilerParams(vmem_limit_bytes=48 * 1024 * 1024),
        cost_estimate=pl.CostEstimate(
            flops=2 * rows * length * columns, bytes_accessed=4 * rows * columns, transcendentals=0
        ),
    )(left, right, *other)


def gate_up_body(hidden, weight, both, activ):
    value = dot(hidden[...], weight[...], 1, 0)
    gate, up = value[:, :TILE], value[:, TILE:]
    sigmoid = jax.nn.sigmoid(gate)
    silu = gate * sigmoid
    activ[...] = (silu * up).astype(bf16)
    both[:, :TILE] = (up * sigmoid * (1.0 + gate * (1.0 - sigmoid))).astype(bf16)
    both[:, TILE:] = silu.astype(bf16)


def gate_up_back_body(grad_mlp, weight, both, out):
    grad = dot(grad_mlp[...], weight[...], 1, 0)
    for start in (0, TILE):
        out[:, start : start + TILE] = (
            grad * both[:, start : start + TILE].astype(f32)
        ).astype(bf16)


def gate_up_kernels(length, width, wide):
    params = pltpu.CompilerParams(vmem_limit_bytes=48 * 1024 * 1024)
    rows_spec = pl.BlockSpec((length, width), lambda j: (0, 0))

    def columns(rows, size):
        return pl.BlockSpec((rows, size), lambda j: (0, j))

    def forward(hidden, weight):
        return pl.pallas_call(
            gate_up_body,
            grid=(wide // TILE,),
            in_specs=[rows_spec, columns(width, 2 * TILE)],
            out_specs=[columns(length, 2 * TILE), columns(length, TILE)],
            out_shape=[
                jax.ShapeDtypeStruct((length, 2 * wide), bf16),
                jax.ShapeDtypeStruct((length, wide), bf16),
            ],
            compiler_params=params,
            cost_estimate=pl.CostEstimate(
                flops=4 * length * width * wide,
                bytes_accessed=10 * length * wide + 4 * width * wide,
                transcendentals=0,
            ),
        )(hidden, weight)

    def backward(grad_mlp, weight, both):
        return pl.pallas_call(
            gate_up_back_body,
            grid=(wide // TILE,),
            in_specs=[rows_spec, columns(width, TILE), columns(length, 2 * TILE)],
            out_specs=columns(length, 2 * TILE),
            out_shape=jax.ShapeDtypeStruct((length, 2 * wide), bf16),
            compiler_params=pltpu.CompilerParams(vmem_limit_bytes=ALL_VMEM),
            cost_estimate=pl.CostEstimate(
                flops=2 * length * width * wide,
                bytes_accessed=12 * length * wide + 2 * width * wide,
                transcendentals=0,
            ),
        )(grad_mlp, weight, both)

    return forward, backward


FSDP, DP = ("y", "x"), ("z", "core")


def order_body(values, other, out):
    pass


def order(values, other):
    anywhere = pl.BlockSpec(memory_space=pl.ANY)
    return pl.pallas_call(
        order_body,
        in_specs=[anywhere, anywhere],
        out_specs=anywhere,
        out_shape=jax.ShapeDtypeStruct(values.shape, values.dtype),
        input_output_aliases={0: 0},
    )(values, other)


def zero_after(other):
    first = other[(slice(0, 1),) * other.ndim].astype(f32).reshape(())
    return jnp.minimum(jnp.abs(first), 0.0).astype(jnp.int32)


class Copies:
    def __init__(self):
        self.count = lax.axis_size("z")

    def swap(self, values):
        return lax.ppermute(values, "core", [(0, 1), (1, 0)])

    def along(self, values):
        return [values] + [
            lax.ppermute(values, "z", [(i, (i + step) % self.count) for i in range(self.count)])
            for step in range(1, self.count)
        ]

    def gather(self, values):
        core, place = lax.axis_index("core"), lax.axis_index("z")
        other = self.swap(values)
        both = jnp.concatenate(
            [lax.select_n(core, values, other), lax.select_n(core, other, values)]
        )
        parts = self.along(both)
        return jnp.concatenate(
            [lax.select_n((place - z) % self.count, *parts) for z in range(self.count)]
        )

    def total(self, values):
        return sum(self.along(values + self.swap(values)))


class Plane:
    def __init__(self, count):
        self.count = count
        self.square = count == 4
        self.place = lax.axis_index(FSDP)

    def swap(self, values, bit):
        return lax.ppermute(values, FSDP, [(i, i ^ bit) for i in range(self.count)])

    def gather(self, block, axis, fill=0):
        if not self.square:
            return lax.all_gather(block, FSDP, axis=axis, tiled=True)
        other = 1 - axis
        size, cut = block.shape[axis], block.shape[other] // 2
        by_x, by_y = self.swap(block, 1), self.swap(block, 2)
        low = self.swap(lax.slice_in_dim(by_x, 0, cut, axis=other), 2)
        high = self.swap(lax.slice_in_dim(by_y, cut, 2 * cut, axis=other), 1)
        shape = list(block.shape)
        shape[axis] = size * 4
        out = jnp.full(shape, fill, block.dtype)
        for part, bit, offset in ((block, 0, 0), (by_x, 1, 0), (by_y, 2, 0), (low, 3, 0), (high, 3, cut)):
            start = [0, 0]
            start[axis] = (self.place ^ bit) * size
            start[other] = offset
            out = lax.dynamic_update_slice(out, part, start)
        return out

    def scatter(self, partial, axis, kind=f32, hop=0, last=(0, 0)):
        if not self.square:
            total = lax.psum_scatter(partial, FSDP, scatter_dimension=axis, tiled=True)
            return total.astype(f32)
        other = 1 - axis
        size, cut = partial.shape[axis] // 4, partial.shape[other] // 2
        place = self.place

        def piece(bit, offset, zero=0):
            start = [0, 0]
            start[axis] = (place ^ bit) * size + zero
            start[other] = offset
            extent = [0, 0]
            extent[axis] = size
            extent[other] = cut
            return lax.dynamic_slice(partial, start, extent)

        halves = []
        for (offset, first, second), zero in zip(((0, 1, 2), (cut, 2, 1)), last):
            relay = self.swap(piece(3, offset), first)
            mine = self.swap(piece(first, offset), first)
            relay = (piece(second, offset, hop).astype(f32) + relay.astype(f32)).astype(bf16)
            halves.append(
                piece(0, offset, zero).astype(f32) + mine.astype(f32) + self.swap(relay, second).astype(f32)
            )
        return jnp.concatenate([half.astype(kind) for half in halves], axis=other)

    def total(self, values):
        if not self.square:
            return lax.psum(values, FSDP)
        return values + self.swap(values, 1) + self.swap(values, 2) + self.swap(values, 3)

    def gather_small(self, values):
        if not self.square:
            return lax.all_gather(values, FSDP, axis=0, tiled=True)
        parts = [values] + [self.swap(values, bit) for bit in (1, 2, 3)]
        return jnp.concatenate(
            [
                lax.select_n(self.place ^ j, *parts)
                for j in range(4)
            ],
            axis=0,
        )


def per_device(
    tokens,
    positions,
    cotangent,
    w_attn,
    w_gate_up,
    w_down,
    gains,
    m_attn,
    v_attn,
    m_gate_up,
    v_gate_up,
    m_down,
    v_down,
    m_gains,
    v_gains,
):
    rows, width = tokens.shape
    owned = w_attn.shape[0]
    hidden = w_down.shape[1]
    count = lax.axis_size(FSDP)
    plane = Plane(count)
    place = plane.place
    length = rows * count
    part = width // count
    heads = part // HEAD_DIM
    wide = hidden // count
    scale = 1.0 / math.sqrt(HEAD_DIM)

    def spread(weight, groups, tile=0):
        block = spread_kernel(weight, groups, count, tile)
        return lax.all_to_all(block, FSDP, 0, 0, tiled=True)

    attn_all = lax.all_gather(spread(w_attn, 4), DP, axis=0, tiled=True)
    gate_up_all = lax.all_gather(spread(w_gate_up, 2, tile=TILE), DP, axis=0, tiled=True)
    down_all = lax.all_gather(spread(w_down, 1), DP, axis=0, tiled=True)
    qkv_weight = attn_all[:, : 3 * part]
    out_weight = attn_all[:, 3 * part : 4 * part]
    copies = Copies()
    gain_low = lax.reduce_precision(gains, exponent_bits=8, mantissa_bits=7)
    gain_values = copies.gather(plane.gather_small(jnp.transpose(gain_low).reshape(-1)))
    gain_values = jnp.transpose(gain_values.reshape(-1, 4, owned), (0, 2, 1)).reshape(width, 4)
    gain_part = lax.dynamic_slice_in_dim(gain_values, place * part, part, 0)

    token_full = plane.gather(tokens, 0)
    position_full = plane.gather_small(positions)
    cot_part = lax.all_to_all(
        cotangent.reshape(rows, count, part).transpose(1, 0, 2).reshape(count * rows, part),
        FSDP,
        0,
        0,
        tiled=True,
    ).astype(f32)

    half_dim = HEAD_DIM // 2
    frequency = jnp.exp(
        jnp.arange(half_dim, dtype=f32) * (-2.0 * math.log(rope_base) / HEAD_DIM)
    )
    angles = position_full.astype(f32)[:, None] * frequency[None, :]
    cosine, sine = jnp.cos(angles), jnp.sin(angles)
    cosine = jnp.concatenate([cosine, cosine], axis=1)
    sine = jnp.concatenate([-sine, sine], axis=1)
    first_key = (jnp.arange(length, dtype=jnp.int32) - position_full)[:, None]
    gain_rows = jnp.pad(jnp.transpose(gain_part), ((0, 4), (0, 0)))
    attend, attend_back = attend_kernels(length, heads)

    qkv = mm(token_full, qkv_weight, ((1,), (0,)))
    query_raw, key_raw = qkv[:, :part], qkv[:, part : 2 * part]
    squares = plane.total(
        jnp.concatenate([jnp.sum(query_raw * query_raw, axis=1), jnp.sum(key_raw * key_raw, axis=1)])
    )
    inverse = jnp.transpose(lax.rsqrt(squares / width + norm_eps).reshape(2, length))
    tables = (inverse, gain_rows, cosine, sine, first_key)
    query, key, value, attended_low, lse = attend(qkv, *tables)
    attended_full = plane.gather(attended_low, 1, 1)

    branch = mm(attended_full, out_weight, ((1,), (0,)))
    branch_inv = lax.rsqrt(plane.total(jnp.sum(branch * branch, axis=1)) / width + norm_eps)[:, None]
    branch_hat = branch * branch_inv
    token_part = lax.dynamic_slice_in_dim(token_full, place * part, part, 1).astype(f32)
    hidden_low = (token_part + branch_hat * gain_part[None, :, 2]).astype(bf16)
    hidden_full = plane.gather(hidden_low, 1, 2)

    core = lax.axis_index("core")
    share = width // (2 * copies.count)

    def sides(array):
        return [
            jnp.transpose(
                jnp.concatenate(
                    [
                        lax.dynamic_slice_in_dim(array, (2 * z + index) * share, share, 1)
                        for z in range(copies.count)
                    ],
                    axis=1,
                )
            )
            for index in (1 - core, core)
        ]

    other_side, own_side = sides(hidden_full)
    token_sides, attended_sides = sides(token_full), sides(attended_full)
    for early in (other_side, own_side, *token_sides, *attended_sides, cot_part):
        hidden_full = order(hidden_full, early)
    gate_up, gate_up_back = gate_up_kernels(length, width, wide)
    both, activ = gate_up(hidden_full, gate_up_all)
    mlp = plane.scatter(mm(activ, down_all, ((1,), (1,))).astype(bf16), 0)
    mlp_inv = lax.rsqrt(jnp.mean(mlp * mlp, axis=1, keepdims=True) + norm_eps)
    mlp_hat = mlp * mlp_inv
    hidden_rows = lax.dynamic_slice_in_dim(hidden_full, place * rows, rows, 0).astype(f32)
    output = (hidden_rows + mlp_hat * gain_values[None, :, 3]).astype(bf16)

    grad_out = cotangent.astype(f32)
    scaled = grad_out * gain_values[None, :, 3]
    grad_mlp = mlp_inv * (scaled - mlp_hat * jnp.mean(scaled * mlp_hat, axis=1, keepdims=True))
    grad_gain_mlp = jnp.sum(grad_out * mlp_hat, axis=0)
    by_rows = Layout(major_to_minor=(0, 1))
    grad_mlp_full = with_layout_constraint(
        plane.gather(with_layout_constraint(grad_mlp.astype(bf16), by_rows), 0, 3), by_rows
    )

    def exchanged(mine, *wait):
        for other in wait:
            mine = order(mine, other)
        return lax.all_to_all(mine, FSDP, 0, 0, tiled=True)

    down_partial = mm(grad_mlp_full, activ, ((0,), (0,))).astype(bf16)
    down_mine = lax.psum_scatter(down_partial, DP, scatter_dimension=0, tiled=True)
    grad_gate_up_low = gate_up_back(grad_mlp_full, down_all, both)

    send = half_grad(other_side, grad_gate_up_low)
    got = copies.swap(send)
    late = order(grad_gate_up_low, send)
    hidden_partial = mm(late, gate_up_all, ((1,), (1,))).astype(bf16)
    grad_hidden = cot_part + plane.scatter(hidden_partial, 1)
    gate_up_partial = half_grad(order(own_side, hidden_partial[:16, :128]), late, got)
    gate_up_mine = lax.psum_scatter(gate_up_partial, "z", scatter_dimension=0, tiled=True)

    scaled = grad_hidden * gain_part[None, :, 2]
    grad_gain_attn = jnp.sum(grad_hidden * branch_hat, axis=0)
    inner = plane.total(jnp.sum(scaled * branch_hat, axis=1))[:, None] / width
    grad_branch = (branch_inv * (scaled - branch_hat * inner)).astype(bf16)
    grad_branch = order(grad_branch, down_mine)
    grad_att = plane.scatter(
        mm(grad_branch, out_weight, ((1,), (1,))).astype(bf16), 1, bf16
    )
    query_grad, key_grad, value_grad, gain_grad, inner = attend_back(
        query, key, value, attended_low, grad_att, lse, qkv, *tables
    )
    inner = plane.total(jnp.concatenate([inner[:, 0], inner[:, 1]])) / width
    inner = jnp.transpose(inner.reshape(2, length))
    grad_qkv_low = qkv_back(query_grad, key_grad, value_grad, qkv, inverse, inner)

    own_gains = jnp.stack([gain_grad[0], gain_grad[1], grad_gain_attn])
    gain_sums = jnp.concatenate([jnp.zeros((3, width), f32), grad_gain_mlp[None]])
    gain_sums = lax.dynamic_update_slice(gain_sums, own_gains, (0, place * part)).reshape(-1)
    gain_sums = plane.total(copies.total(gain_sums)).reshape(4, width)
    owner = lax.axis_index(DP + FSDP)
    grad_gains = jnp.transpose(lax.dynamic_slice_in_dim(gain_sums, owner * owned, owned, 1))
    send = attn_grad(token_sides[0], grad_qkv_low, attended_sides[0], grad_branch)
    got = copies.swap(send)
    late = order(grad_qkv_low, send)
    back = token_grad(jnp.full((1,), place), late, attn_all, grad_hidden)
    late = order(late, back)
    attn_partial = attn_grad(token_sides[1], late, attended_sides[1], grad_branch, got)
    down_part = exchanged(down_mine, grad_qkv_low)
    attn_partial = order(order(attn_partial, down_part), gate_up_mine)
    attn_mine = lax.psum_scatter(attn_partial, "z", scatter_dimension=0, tiled=True)
    gate_up_part = exchanged(gate_up_mine, attn_partial)
    grad_down, new_down, new_m_down, new_v_down = adamw_kernel(
        order(down_part, attn_partial), w_down, m_down, v_down, 1, count
    )
    grad_tokens = plane.scatter(
        back,
        0,
        hop=zero_after(new_down),
        last=(zero_after(gate_up_part), zero_after(grad_gains)),
    )
    attn_mine = order(order(attn_mine, grad_tokens), new_down)
    attn_part = exchanged(attn_mine)
    grad_gate_up, new_gate_up, new_m_gate_up, new_v_gate_up = adamw_kernel(
        order(gate_up_part, attn_mine), w_gate_up, m_gate_up, v_gate_up, 2, count, TILE
    )
    grad_attn, new_attn, new_m_attn, new_v_attn = adamw_kernel(
        order(attn_part, new_gate_up), w_attn, m_attn, v_attn, 4, count
    )
    new_gains, new_m_gains, new_v_gains = adamw_step(
        gains, grad_gains, m_gains, v_gains, 0.0, gain_rate
    )
    return (
        output,
        grad_tokens,
        grad_attn,
        grad_gate_up,
        grad_down,
        grad_gains,
        new_attn,
        new_gate_up,
        new_down,
        new_gains,
        new_m_attn,
        new_v_attn,
        new_m_gate_up,
        new_v_gate_up,
        new_m_down,
        new_v_down,
        new_m_gains,
        new_v_gains,
    )


def solution(mesh):
    copies, places = mesh.devices.shape
    mesh = Mesh(mesh.devices.reshape(copies // 2, 2, 2, places // 2), DP + FSDP)
    matrix, vector = P(DP + FSDP, None), P(DP + FSDP)
    in_specs = (matrix, vector) + (matrix,) * 13
    return jax.shard_map(
        per_device, mesh=mesh, in_specs=in_specs, out_specs=(matrix,) * 18, check_vma=False
    )
```

```python
import functools
import math

import jax
import jax.numpy as jnp
from jax import lax
from jax.experimental import pallas as pl
from jax.experimental.pallas import tpu as pltpu
from jax.experimental.layout import Layout, with_layout_constraint
from jax.sharding import Mesh
from jax.sharding import PartitionSpec as P

HEAD_DIM = 128

norm_eps = 1e-06
rope_base = 500000.0
learn_rate = 0.004
gain_rate = 0.25
beta_one = 0.9
beta_two = 0.95
decay_rate = 0.1
adam_eps = 1e-08
correct_one = 1.0 - beta_one**2
correct_two = 1.0 - beta_two**2
neg_large = -1e30
bf16 = jnp.bfloat16
f32 = jnp.float32
TILE = 512
ALL_VMEM = 60 * 1024 * 1024


def mm(left, right, dims):
    return lax.dot_general(left, right, (dims, ((), ())), preferred_element_type=f32)


def adamw_step(weight, gradient, moment, second, decay_coef, rate_value):
    moment_new = beta_one * moment + (1.0 - beta_one) * gradient
    second_new = beta_two * second + (1.0 - beta_two) * gradient * gradient
    step_ratio = moment_new / correct_one / (jnp.sqrt(second_new / correct_two) + adam_eps)
    return (
        weight * (1.0 - rate_value * decay_coef) - rate_value * step_ratio,
        moment_new,
        second_new,
    )


def spread_body(tile, *refs):
    out = refs[-1]
    if tile:
        for i in range(refs[0].shape[1] // tile):
            for g, ref in enumerate(refs[:-1]):
                start = (i * len(refs[:-1]) + g) * tile
                out[:, start : start + tile] = ref[:, i * tile : (i + 1) * tile].astype(bf16)
        return
    start = 0
    for ref in refs[:-1]:
        out[:, start : start + ref.shape[1]] = ref[...].astype(bf16)
        start += ref.shape[1]


def spread_kernel(weight, groups, count, tile):
    owned, columns = weight.shape
    size = columns // (groups * count)
    specs = [
        pl.BlockSpec((owned, size), lambda f, g=g: (0, g * count + f)) for g in range(groups)
    ]
    operands = [weight] * groups
    wide = groups * size
    return pl.pallas_call(
        functools.partial(spread_body, tile),
        grid=(count,),
        in_specs=specs,
        out_specs=pl.BlockSpec((owned, wide), lambda f: (f, 0)),
        out_shape=jax.ShapeDtypeStruct((count * owned, wide), bf16),
        compiler_params=pltpu.CompilerParams(vmem_limit_bytes=40 * 1024 * 1024),
        cost_estimate=pl.CostEstimate(
            flops=0, bytes_accessed=6 * owned * columns, transcendentals=0
        ),
    )(*operands)


def adamw_body(tile, *refs):
    grad_in, weight, moment, second, grad_out, new_weight, new_moment, new_second = refs
    if tile:
        groups = grad_in.shape[1] // weight.shape[1]
        for i in range(weight.shape[1] // tile):
            start = pl.multiple_of((i * groups + pl.program_id(1)) * tile, tile)
            grad_out[:, i * tile : (i + 1) * tile] = grad_in[:, pl.ds(start, tile)].astype(f32)
    else:
        grad_out[...] = grad_in[...].astype(f32)
    new_weight[...], new_moment[...], new_second[...] = adamw_step(
        weight[...], grad_out[...], moment[...], second[...], decay_rate, learn_rate
    )


def adamw_kernel(gradient, weight, moment, second, groups, count, tile=0):
    owned, columns = weight.shape
    size = columns // (groups * count)
    whole = pl.BlockSpec((owned, size), lambda f, g: (0, g * count + f))
    if tile:
        grad_spec = pl.BlockSpec((owned, groups * size), lambda f, g: (f, 0))
    else:
        grad_spec = pl.BlockSpec((owned, size), lambda f, g: (f, g))
    return pl.pallas_call(
        functools.partial(adamw_body, tile),
        grid=(count, groups),
        in_specs=[grad_spec, whole, whole, whole],
        out_specs=[whole] * 4,
        out_shape=[jax.ShapeDtypeStruct(weight.shape, f32)] * 4,
        compiler_params=pltpu.CompilerParams(vmem_limit_bytes=40 * 1024 * 1024),
        cost_estimate=pl.CostEstimate(
            flops=12 * owned * columns, bytes_accessed=30 * owned * columns, transcendentals=0
        ),
    )(gradient, weight, moment, second)


def dot(left, right, left_dim, right_dim):
    return lax.dot_general(
        left, right, (((left_dim,), (right_dim,)), ((), ())), preferred_element_type=f32
    )


def visible(first_ref, low, high):
    shape = (high - low, high)
    row = lax.broadcasted_iota(jnp.int32, shape, 0) + low
    column = lax.broadcasted_iota(jnp.int32, shape, 1)
    return (column <= row) & (column >= first_ref[low:high, :])


def attend_body(block, scale, *refs):
    query_in, key_in, value_in, inverse, gain, cosine, sine, first = refs[:8]
    query_out, key_out, value_out, attended, lse = refs[8:]

    def turned(values, column):
        normed = values * inverse[:, column : column + 1] * gain[column : column + 1, :]
        return (normed * cosine[...] + pltpu.roll(normed, HEAD_DIM // 2, 1) * sine[...]).astype(bf16)

    query_out[...] = turned(query_in[...], 0)
    key_out[...] = turned(key_in[...], 1)
    value_out[...] = value_in[...].astype(bf16)
    for low in range(0, query_in.shape[0], block):
        high = low + block
        scores = dot(query_out[low:high, :], key_out[:high, :], 1, 1) * scale
        scores = jnp.where(visible(first, low, high), scores, neg_large)
        top = jnp.max(scores, axis=1, keepdims=True)
        weights = jnp.exp(scores - top)
        denom = jnp.sum(weights, axis=1, keepdims=True)
        attended[low:high, :] = (
            dot(weights.astype(bf16), value_out[:high, :], 1, 0) / denom
        ).astype(bf16)
        lse[0, low:high, :] = top + jnp.log(denom)


def attend_back_body(block, scale, *refs):
    query, key, value, attended, grad_att, lse = refs[:6]
    query_in, key_in, inverse, gain, cosine, sine, first = refs[6:13]
    query_grad, key_grad, value_grad, gain_grad, inner = refs[13:18]
    key_sum, value_sum = refs[18:]
    grad_low = grad_att
    delta = jnp.sum(
        grad_low[...].astype(f32) * attended[...].astype(f32), axis=1, keepdims=True
    )
    key_sum[...] = jnp.zeros_like(key_sum)
    value_sum[...] = jnp.zeros_like(value_sum)
    for low in range(0, query.shape[0], block):
        high = low + block
        scores = dot(query[low:high, :], key[:high, :], 1, 1) * scale
        prob = jnp.where(
            visible(first, low, high), jnp.exp(scores - lse[0, low:high, :]), 0.0
        )
        grad_prob = dot(grad_low[low:high, :], value[:high, :], 1, 1)
        grad_scores = (prob * (grad_prob - delta[low:high, :])).astype(bf16)
        query_grad[low:high, :] = dot(grad_scores, key[:high, :], 1, 0) * scale
        key_sum[:high, :] += dot(grad_scores, query[low:high, :], 0, 0)
        value_sum[:high, :] += dot(prob.astype(bf16), grad_low[low:high, :], 0, 0)
    value_grad[...] = value_sum[...].astype(bf16)
    lane = lax.broadcasted_iota(jnp.int32, inner.shape, 1)

    @pl.when(pl.program_id(0) == 0)
    def _():
        inner[...] = jnp.zeros_like(inner)

    gain_grad[...] = jnp.zeros_like(gain_grad)
    for column, turned, raw, out in (
        (0, query_grad[...], query_in, query_grad),
        (1, key_sum[...] * scale, key_in, key_grad),
    ):
        back = turned * cosine[...] - pltpu.roll(turned, HEAD_DIM // 2, 1) * sine[...]
        hat = raw[...] * inverse[:, column : column + 1]
        gain_grad[column : column + 1, :] = jnp.sum(back * hat, axis=0, keepdims=True)
        back = back * gain[column : column + 1, :]
        out[...] = back
        inner[...] += jnp.where(
            lane == column, jnp.sum(back * hat, axis=1, keepdims=True), 0.0
        )


def attend_kernels(length, heads):
    block = math.gcd(length, 256)
    scale = 1.0 / math.sqrt(HEAD_DIM)
    part = heads * HEAD_DIM

    def own(shift=0):
        return pl.BlockSpec((length, HEAD_DIM), lambda h: (0, h + shift))

    def same(width):
        return pl.BlockSpec((length, width), lambda h: (0, 0))

    gain_spec = pl.BlockSpec((8, HEAD_DIM), lambda h: (0, h))
    lse_spec = pl.BlockSpec((1, length, 1), lambda h: (h, 0, 0))
    tables = [same(2), gain_spec, same(HEAD_DIM), same(HEAD_DIM), same(1)]
    low_shape = jax.ShapeDtypeStruct((length, part), bf16)
    wide_shape = jax.ShapeDtypeStruct((length, part), f32)
    work = 2 * heads * length * length * HEAD_DIM
    params = pltpu.CompilerParams(vmem_limit_bytes=48 * 1024 * 1024)

    def forward(qkv, *rest):
        return pl.pallas_call(
            functools.partial(attend_body, block, scale),
            grid=(heads,),
            in_specs=[own(), own(heads), own(2 * heads)] + tables,
            out_specs=[own()] * 4 + [lse_spec],
            out_shape=[low_shape] * 4 + [jax.ShapeDtypeStruct((heads, length, 1), f32)],
            compiler_params=params,
            cost_estimate=pl.CostEstimate(
                flops=2 * work, bytes_accessed=20 * length * part, transcendentals=0
            ),
        )(qkv, qkv, qkv, *rest)

    def backward(query, key, value, attended, grad_att, lse, qkv, *rest):
        return pl.pallas_call(
            functools.partial(attend_back_body, block, scale),
            grid=(heads,),
            in_specs=[own()] * 5 + [lse_spec, own(), own(heads)] + tables,
            out_specs=[own()] * 3 + [gain_spec, same(HEAD_DIM)],
            out_shape=[
                wide_shape,
                wide_shape,
                low_shape,
                jax.ShapeDtypeStruct((8, part), f32),
                jax.ShapeDtypeStruct((length, HEAD_DIM), f32),
            ],
            scratch_shapes=[
                pltpu.VMEM((length, HEAD_DIM), f32),
                pltpu.VMEM((length, HEAD_DIM), f32),
            ],
            compiler_params=params,
            cost_estimate=pl.CostEstimate(
                flops=5 * work, bytes_accessed=30 * length * part, transcendentals=0
            ),
        )(query, key, value, attended, grad_att, lse, qkv, qkv, *rest)

    return forward, backward


def qkv_back_body(query_grad, key_grad, value_grad, raw, inverse, inner, out):
    part = query_grad.shape[1]
    for column, grad in ((0, query_grad), (1, key_grad)):
        scale = inverse[:, column : column + 1]
        hat = raw[:, column * part : (column + 1) * part] * scale
        out[:, column * part : (column + 1) * part] = (
            scale * (grad[...] - hat * inner[:, column : column + 1])
        ).astype(bf16)
    out[:, 2 * part :] = value_grad[...]


def qkv_back(query_grad, key_grad, value_grad, qkv, inverse, inner):
    length, part = query_grad.shape
    rows = math.gcd(length, 256)

    def spec(width):
        return pl.BlockSpec((rows, width), lambda i: (i, 0))

    return pl.pallas_call(
        qkv_back_body,
        grid=(length // rows,),
        in_specs=[spec(part)] * 3 + [spec(2 * part), spec(2), spec(2)],
        out_specs=spec(3 * part),
        out_shape=jax.ShapeDtypeStruct((length, 3 * part), bf16),
        compiler_params=pltpu.CompilerParams(vmem_limit_bytes=ALL_VMEM),
        cost_estimate=pl.CostEstimate(
            flops=8 * length * part, bytes_accessed=24 * length * part, transcendentals=0
        ),
    )(query_grad, key_grad, value_grad, qkv, inverse, inner)


def attn_grad_body(token, grad_qkv, attended, grad_branch, *rest):
    out = rest[-1]
    wide = grad_qkv.shape[1]
    for low, high, left, right in (
        (0, wide, token, grad_qkv),
        (wide, out.shape[1], attended, grad_branch),
    ):
        value = dot(left[...], right[...], 1, 0)
        if len(rest) > 1:
            value = value + rest[0][:, low:high].astype(f32)
        out[:, low:high] = value.astype(bf16)


def attn_grad(token, grad_qkv, attended, grad_branch, *other):
    width, length = token.shape
    rows = math.gcd(width, 512)
    columns = grad_qkv.shape[1] + grad_branch.shape[1]

    def row_spec(wide):
        return pl.BlockSpec((rows, wide), lambda i: (i, 0))

    def whole(array):
        return pl.BlockSpec(array.shape, lambda i: (0, 0))

    return pl.pallas_call(
        attn_grad_body,
        grid=(width // rows,),
        in_specs=[row_spec(length), whole(grad_qkv), row_spec(length), whole(grad_branch)]
        + [row_spec(columns)] * len(other),
        out_specs=row_spec(columns),
        out_shape=jax.ShapeDtypeStruct((width, columns), bf16),
        compiler_params=pltpu.CompilerParams(vmem_limit_bytes=ALL_VMEM),
        cost_estimate=pl.CostEstimate(
            flops=2 * width * length * columns,
            bytes_accessed=6 * width * length,
            transcendentals=0,
        ),
    )(token, grad_qkv, attended, grad_branch, *other)


def token_grad_body(place, grad_qkv, weight, grad_hidden, out):
    own = (pl.program_id(0) == place[0]).astype(f32)
    out[...] = (dot(grad_qkv[...], weight[...], 1, 1) + own * grad_hidden[...]).astype(bf16)


def token_grad(place, grad_qkv, weight, grad_hidden):
    length, wide = grad_qkv.shape
    width, part = weight.shape[0], grad_hidden.shape[1]
    return pl.pallas_call(
        token_grad_body,
        grid_spec=pltpu.PrefetchScalarGridSpec(
            num_scalar_prefetch=1,
            grid=(width // part,),
            in_specs=[
                pl.BlockSpec((length, wide), lambda j, place: (0, 0)),
                pl.BlockSpec((part, wide), lambda j, place: (j, 0)),
                pl.BlockSpec((length, part), lambda j, place: (0, 0)),
            ],
            out_specs=pl.BlockSpec((length, part), lambda j, place: (0, j)),
        ),
        out_shape=jax.ShapeDtypeStruct((length, width), bf16),
        compiler_params=pltpu.CompilerParams(vmem_limit_bytes=ALL_VMEM),
        cost_estimate=pl.CostEstimate(
            flops=2 * width * length * wide, bytes_accessed=8 * width * length, transcendentals=0
        ),
    )(place, grad_qkv, weight, grad_hidden)


def half_grad_body(left, right, *rest):
    value = dot(left[...], right[...], 1, 0)
    if len(rest) > 1:
        value = value + rest[0][...].astype(f32)
    rest[-1][...] = value.astype(bf16)


def half_grad(left, right, *other):
    rows, length = left.shape
    columns = right.shape[1]
    size = math.gcd(columns, 512)
    spec = pl.BlockSpec((rows, size), lambda j: (0, j))
    return pl.pallas_call(
        half_grad_body,
        grid=(columns // size,),
        in_specs=[
            pl.BlockSpec((rows, length), lambda j: (0, 0)),
            pl.BlockSpec((length, size), lambda j: (0, j)),
        ]
        + [spec] * len(other),
        out_specs=spec,
        out_shape=jax.ShapeDtypeStruct((rows, columns), bf16),
        compiler_params=pltpu.CompilerParams(vmem_limit_bytes=ALL_VMEM),
        cost_estimate=pl.CostEstimate(
            flops=2 * rows * length * columns, bytes_accessed=4 * rows * columns, transcendentals=0
        ),
    )(left, right, *other)


def gate_up_body(hidden, weight, both, activ):
    value = dot(hidden[...], weight[...], 1, 0)
    gate, up = value[:, :TILE], value[:, TILE:]
    sigmoid = jax.nn.sigmoid(gate)
    silu = gate * sigmoid
    activ[...] = (silu * up).astype(bf16)
    both[:, :TILE] = (up * sigmoid * (1.0 + gate * (1.0 - sigmoid))).astype(bf16)
    both[:, TILE:] = silu.astype(bf16)


def gate_up_back_body(grad_mlp, weight, both, out):
    grad = dot(grad_mlp[...], weight[...], 1, 0)
    for start in (0, TILE):
        out[:, start : start + TILE] = (
            grad * both[:, start : start + TILE].astype(f32)
        ).astype(bf16)


def gate_up_kernels(length, width, wide):
    params = pltpu.CompilerParams(vmem_limit_bytes=48 * 1024 * 1024)
    rows_spec = pl.BlockSpec((length, width), lambda j: (0, 0))

    def columns(rows, size):
        return pl.BlockSpec((rows, size), lambda j: (0, j))

    def forward(hidden, weight):
        return pl.pallas_call(
            gate_up_body,
            grid=(wide // TILE,),
            in_specs=[rows_spec, columns(width, 2 * TILE)],
            out_specs=[columns(length, 2 * TILE), columns(length, TILE)],
            out_shape=[
                jax.ShapeDtypeStruct((length, 2 * wide), bf16),
                jax.ShapeDtypeStruct((length, wide), bf16),
            ],
            compiler_params=params,
            cost_estimate=pl.CostEstimate(
                flops=4 * length * width * wide,
                bytes_accessed=10 * length * wide + 4 * width * wide,
                transcendentals=0,
            ),
        )(hidden, weight)

    def backward(grad_mlp, weight, both):
        return pl.pallas_call(
            gate_up_back_body,
            grid=(wide // TILE,),
            in_specs=[rows_spec, columns(width, TILE), columns(length, 2 * TILE)],
            out_specs=columns(length, 2 * TILE),
            out_shape=jax.ShapeDtypeStruct((length, 2 * wide), bf16),
            compiler_params=pltpu.CompilerParams(vmem_limit_bytes=ALL_VMEM),
            cost_estimate=pl.CostEstimate(
                flops=2 * length * width * wide,
                bytes_accessed=12 * length * wide + 2 * width * wide,
                transcendentals=0,
            ),
        )(grad_mlp, weight, both)

    return forward, backward


FSDP, DP = ("y", "x"), ("z", "core")


def order_body(values, other, out):
    pass


def order(values, other):
    anywhere = pl.BlockSpec(memory_space=pl.ANY)
    return pl.pallas_call(
        order_body,
        in_specs=[anywhere, anywhere],
        out_specs=anywhere,
        out_shape=jax.ShapeDtypeStruct(values.shape, values.dtype),
        input_output_aliases={0: 0},
    )(values, other)


def zero_after(other):
    first = other[(slice(0, 1),) * other.ndim].astype(f32).reshape(())
    return jnp.minimum(jnp.abs(first), 0.0).astype(jnp.int32)


class Copies:
    def __init__(self):
        self.count = lax.axis_size("z")

    def swap(self, values):
        return lax.ppermute(values, "core", [(0, 1), (1, 0)])

    def along(self, values):
        return [values] + [
            lax.ppermute(values, "z", [(i, (i + step) % self.count) for i in range(self.count)])
            for step in range(1, self.count)
        ]

    def gather(self, values):
        core, place = lax.axis_index("core"), lax.axis_index("z")
        other = self.swap(values)
        both = jnp.concatenate(
            [lax.select_n(core, values, other), lax.select_n(core, other, values)]
        )
        parts = self.along(both)
        return jnp.concatenate(
            [lax.select_n((place - z) % self.count, *parts) for z in range(self.count)]
        )

    def total(self, values):
        return sum(self.along(values + self.swap(values)))


class Plane:
    def __init__(self, count):
        self.count = count
        self.square = count == 4
        self.place = lax.axis_index(FSDP)

    def swap(self, values, bit):
        return lax.ppermute(values, FSDP, [(i, i ^ bit) for i in range(self.count)])

    def gather(self, block, axis, fill=0):
        if not self.square:
            return lax.all_gather(block, FSDP, axis=axis, tiled=True)
        other = 1 - axis
        size, cut = block.shape[axis], block.shape[other] // 2
        by_x, by_y = self.swap(block, 1), self.swap(block, 2)
        low = self.swap(lax.slice_in_dim(by_x, 0, cut, axis=other), 2)
        high = self.swap(lax.slice_in_dim(by_y, cut, 2 * cut, axis=other), 1)
        shape = list(block.shape)
        shape[axis] = size * 4
        out = jnp.full(shape, fill, block.dtype)
        for part, bit, offset in ((block, 0, 0), (by_x, 1, 0), (by_y, 2, 0), (low, 3, 0), (high, 3, cut)):
            start = [0, 0]
            start[axis] = (self.place ^ bit) * size
            start[other] = offset
            out = lax.dynamic_update_slice(out, part, start)
        return out

    def scatter(self, partial, axis, kind=f32, hop=0, last=(0, 0)):
        if not self.square:
            total = lax.psum_scatter(partial, FSDP, scatter_dimension=axis, tiled=True)
            return total.astype(f32)
        other = 1 - axis
        size, cut = partial.shape[axis] // 4, partial.shape[other] // 2
        place = self.place

        def piece(bit, offset, zero=0):
            start = [0, 0]
            start[axis] = (place ^ bit) * size + zero
            start[other] = offset
            extent = [0, 0]
            extent[axis] = size
            extent[other] = cut
            return lax.dynamic_slice(partial, start, extent)

        halves = []
        for (offset, first, second), zero in zip(((0, 1, 2), (cut, 2, 1)), last):
            relay = self.swap(piece(3, offset), first)
            mine = self.swap(piece(first, offset), first)
            relay = (piece(second, offset, hop).astype(f32) + relay.astype(f32)).astype(bf16)
            halves.append(
                piece(0, offset, zero).astype(f32) + mine.astype(f32) + self.swap(relay, second).astype(f32)
            )
        return jnp.concatenate([half.astype(kind) for half in halves], axis=other)

    def total(self, values):
        if not self.square:
            return lax.psum(values, FSDP)
        return values + self.swap(values, 1) + self.swap(values, 2) + self.swap(values, 3)

    def gather_small(self, values):
        if not self.square:
            return lax.all_gather(values, FSDP, axis=0, tiled=True)
        parts = [values] + [self.swap(values, bit) for bit in (1, 2, 3)]
        return jnp.concatenate(
            [
                lax.select_n(self.place ^ j, *parts)
                for j in range(4)
            ],
            axis=0,
        )


def per_device(
    tokens,
    positions,
    cotangent,
    w_attn,
    w_gate_up,
    w_down,
    gains,
    m_attn,
    v_attn,
    m_gate_up,
    v_gate_up,
    m_down,
    v_down,
    m_gains,
    v_gains,
):
    rows, width = tokens.shape
    owned = w_attn.shape[0]
    hidden = w_down.shape[1]
    count = lax.axis_size(FSDP)
    plane = Plane(count)
    place = plane.place
    length = rows * count
    part = width // count
    heads = part // HEAD_DIM
    wide = hidden // count
    scale = 1.0 / math.sqrt(HEAD_DIM)

    def spread(weight, groups, tile=0):
        block = spread_kernel(weight, groups, count, tile)
        return lax.all_to_all(block, FSDP, 0, 0, tiled=True)

    attn_all = lax.all_gather(spread(w_attn, 4), DP, axis=0, tiled=True)
    gate_up_all = lax.all_gather(spread(w_gate_up, 2, tile=TILE), DP, axis=0, tiled=True)
    down_all = lax.all_gather(spread(w_down, 1), DP, axis=0, tiled=True)
    qkv_weight = attn_all[:, : 3 * part]
    out_weight = attn_all[:, 3 * part : 4 * part]
    copies = Copies()
    gain_low = lax.reduce_precision(gains, exponent_bits=8, mantissa_bits=7)
    gain_values = copies.gather(plane.gather_small(jnp.transpose(gain_low).reshape(-1)))
    gain_values = jnp.transpose(gain_values.reshape(-1, 4, owned), (0, 2, 1)).reshape(width, 4)
    gain_part = lax.dynamic_slice_in_dim(gain_values, place * part, part, 0)

    token_full = plane.gather(tokens, 0)
    position_full = plane.gather_small(positions)
    cot_part = lax.all_to_all(
        cotangent.reshape(rows, count, part).transpose(1, 0, 2).reshape(count * rows, part),
        FSDP,
        0,
        0,
        tiled=True,
    ).astype(f32)

    half_dim = HEAD_DIM // 2
    frequency = jnp.exp(
        jnp.arange(half_dim, dtype=f32) * (-2.0 * math.log(rope_base) / HEAD_DIM)
    )
    angles = position_full.astype(f32)[:, None] * frequency[None, :]
    cosine, sine = jnp.cos(angles), jnp.sin(angles)
    cosine = jnp.concatenate([cosine, cosine], axis=1)
    sine = jnp.concatenate([-sine, sine], axis=1)
    first_key = (jnp.arange(length, dtype=jnp.int32) - position_full)[:, None]
    gain_rows = jnp.pad(jnp.transpose(gain_part), ((0, 4), (0, 0)))
    attend, attend_back = attend_kernels(length, heads)

    qkv = mm(token_full, qkv_weight, ((1,), (0,)))
    query_raw, key_raw = qkv[:, :part], qkv[:, part : 2 * part]
    squares = plane.total(
        jnp.concatenate([jnp.sum(query_raw * query_raw, axis=1), jnp.sum(key_raw * key_raw, axis=1)])
    )
    inverse = jnp.transpose(lax.rsqrt(squares / width + norm_eps).reshape(2, length))
    tables = (inverse, gain_rows, cosine, sine, first_key)
    query, key, value, attended_low, lse = attend(qkv, *tables)
    attended_full = plane.gather(attended_low, 1, 1)

    branch = mm(attended_full, out_weight, ((1,), (0,)))
    branch_inv = lax.rsqrt(plane.total(jnp.sum(branch * branch, axis=1)) / width + norm_eps)[:, None]
    branch_hat = branch * branch_inv
    token_part = lax.dynamic_slice_in_dim(token_full, place * part, part, 1).astype(f32)
    hidden_low = (token_part + branch_hat * gain_part[None, :, 2]).astype(bf16)
    hidden_full = plane.gather(hidden_low, 1, 2)

    core = lax.axis_index("core")
    share = width // (2 * copies.count)

    def sides(array):
        return [
            jnp.transpose(
                jnp.concatenate(
                    [
                        lax.dynamic_slice_in_dim(array, (2 * z + index) * share, share, 1)
                        for z in range(copies.count)
                    ],
                    axis=1,
                )
            )
            for index in (1 - core, core)
        ]

    other_side, own_side = sides(hidden_full)
    token_sides, attended_sides = sides(token_full), sides(attended_full)
    for early in (other_side, own_side, *token_sides, *attended_sides, cot_part):
        hidden_full = order(hidden_full, early)
    gate_up, gate_up_back = gate_up_kernels(length, width, wide)
    both, activ = gate_up(hidden_full, gate_up_all)
    mlp = plane.scatter(mm(activ, down_all, ((1,), (1,))).astype(bf16), 0)
    mlp_inv = lax.rsqrt(jnp.mean(mlp * mlp, axis=1, keepdims=True) + norm_eps)
    mlp_hat = mlp * mlp_inv
    hidden_rows = lax.dynamic_slice_in_dim(hidden_full, place * rows, rows, 0).astype(f32)
    output = (hidden_rows + mlp_hat * gain_values[None, :, 3]).astype(bf16)

    grad_out = cotangent.astype(f32)
    scaled = grad_out * gain_values[None, :, 3]
    grad_mlp = mlp_inv * (scaled - mlp_hat * jnp.mean(scaled * mlp_hat, axis=1, keepdims=True))
    grad_gain_mlp = jnp.sum(grad_out * mlp_hat, axis=0)
    by_rows = Layout(major_to_minor=(0, 1))
    grad_mlp_full = with_layout_constraint(
        plane.gather(with_layout_constraint(grad_mlp.astype(bf16), by_rows), 0, 3), by_rows
    )

    def exchanged(mine, *wait):
        for other in wait:
            mine = order(mine, other)
        return lax.all_to_all(mine, FSDP, 0, 0, tiled=True)

    down_partial = mm(grad_mlp_full, activ, ((0,), (0,))).astype(bf16)
    down_mine = lax.psum_scatter(down_partial, DP, scatter_dimension=0, tiled=True)
    grad_gate_up_low = gate_up_back(grad_mlp_full, down_all, both)

    send = half_grad(other_side, grad_gate_up_low)
    got = copies.swap(send)
    late = order(grad_gate_up_low, send)
    hidden_partial = mm(late, gate_up_all, ((1,), (1,))).astype(bf16)
    grad_hidden = cot_part + plane.scatter(hidden_partial, 1)
    gate_up_partial = half_grad(order(own_side, hidden_partial[:16, :128]), late, got)
    gate_up_mine = lax.psum_scatter(gate_up_partial, "z", scatter_dimension=0, tiled=True)

    scaled = grad_hidden * gain_part[None, :, 2]
    grad_gain_attn = jnp.sum(grad_hidden * branch_hat, axis=0)
    inner = plane.total(jnp.sum(scaled * branch_hat, axis=1))[:, None] / width
    grad_branch = (branch_inv * (scaled - branch_hat * inner)).astype(bf16)
    grad_branch = order(grad_branch, down_mine)
    grad_att = plane.scatter(
        mm(grad_branch, out_weight, ((1,), (1,))).astype(bf16), 1, bf16
    )
    query_grad, key_grad, value_grad, gain_grad, inner = attend_back(
        query, key, value, attended_low, grad_att, lse, qkv, *tables
    )
    inner = plane.total(jnp.concatenate([inner[:, 0], inner[:, 1]])) / width
    inner = jnp.transpose(inner.reshape(2, length))
    grad_qkv_low = qkv_back(query_grad, key_grad, value_grad, qkv, inverse, inner)

    own_gains = jnp.stack([gain_grad[0], gain_grad[1], grad_gain_attn])
    gain_sums = jnp.concatenate([jnp.zeros((3, width), f32), grad_gain_mlp[None]])
    gain_sums = lax.dynamic_update_slice(gain_sums, own_gains, (0, place * part)).reshape(-1)
    gain_sums = plane.total(copies.total(gain_sums)).reshape(4, width)
    owner = lax.axis_index(DP + FSDP)
    grad_gains = jnp.transpose(lax.dynamic_slice_in_dim(gain_sums, owner * owned, owned, 1))
    send = attn_grad(token_sides[0], grad_qkv_low, attended_sides[0], grad_branch)
    got = copies.swap(send)
    late = order(grad_qkv_low, send)
    back = token_grad(jnp.full((1,), place), late, attn_all, grad_hidden)
    late = order(late, back)
    attn_partial = attn_grad(token_sides[1], late, attended_sides[1], grad_branch, got)
    down_part = exchanged(down_mine, grad_qkv_low)
    attn_partial = order(order(attn_partial, down_part), gate_up_mine)
    attn_mine = lax.psum_scatter(attn_partial, "z", scatter_dimension=0, tiled=True)
    gate_up_part = exchanged(gate_up_mine, attn_partial)
    grad_down, new_down, new_m_down, new_v_down = adamw_kernel(
        order(down_part, attn_partial), w_down, m_down, v_down, 1, count
    )
    grad_tokens = plane.scatter(
        back,
        0,
        hop=zero_after(new_down),
        last=(zero_after(gate_up_part), zero_after(grad_gains)),
    )
    attn_mine = order(order(attn_mine, grad_tokens), new_down)
    attn_part = exchanged(attn_mine)
    grad_gate_up, new_gate_up, new_m_gate_up, new_v_gate_up = adamw_kernel(
        order(gate_up_part, attn_mine), w_gate_up, m_gate_up, v_gate_up, 2, count, TILE
    )
    grad_attn, new_attn, new_m_attn, new_v_attn = adamw_kernel(
        order(attn_part, new_gate_up), w_attn, m_attn, v_attn, 4, count
    )
    new_gains, new_m_gains, new_v_gains = adamw_step(
        gains, grad_gains, m_gains, v_gains, 0.0, gain_rate
    )
    return (
        output,
        grad_tokens,
        grad_attn,
        grad_gate_up,
        grad_down,
        grad_gains,
        new_attn,
        new_gate_up,
        new_down,
        new_gains,
        new_m_attn,
        new_v_attn,
        new_m_gate_up,
        new_v_gate_up,
        new_m_down,
        new_v_down,
        new_m_gains,
        new_v_gains,
    )


def solution(mesh):
    copies, places = mesh.devices.shape
    mesh = Mesh(mesh.devices.reshape(copies // 2, 2, 2, places // 2), DP + FSDP)
    matrix, vector = P(DP + FSDP, None), P(DP + FSDP)
    in_specs = (matrix, vector) + (matrix,) * 13
    return jax.shard_map(
        per_device, mesh=mesh, in_specs=in_specs, out_specs=(matrix,) * 18, check_vma=False
    )
```
